256 devices in a mesh: dp: 16 (over z, core), tensor: 16 (over x, y).
Axes of the slice: x: 4, y: 4, z: 8, core: 2. Of those that a mesh axis runs over, the one named last changes fastest.
Arguments:
- gate_pre: bfloat16 [16384, 14336], P('dp', 'tensor'), may hold values from -6 to 6
- up_pre: bfloat16 [16384, 14336], P('dp', 'tensor'), may hold values from -6 to 6
- grad_out: bfloat16 [16384, 4096], P(('dp', 'tensor')), may hold values from -0.59765625 to 0.59765625
- error: bfloat16 [16, 14336, 4096], P('dp', 'tensor'), may hold values from -3 to 3
- sketch: float32 [32, 4096], replicated, may hold values from -6 to 6
Outputs:
- p_factor: float32 [32, 14336], P(None, 'tensor')
- q_factor: float32 [16, 32, 4096], P('tensor')
The draws below stay inside these ranges and needn't reach their ends.
All inputs are finite; a program needn't handle non-finite values.
Results may differ from the reference program's by a relative error of at most 0.0035.
Values may be sent and summed in bfloat16 or wider, within the bound.
A program may use at most 128 MiB of HBM per device.

```python
import jax
import jax.numpy as jnp
from jax import lax

D = 4096
FF = 14336
TOK = 1024
R = 32
REPLICAS = 16
TOKENS = 16384
N_DP = 16
N_TENSOR = 16


def block_scale(rng, extent, pieces, low, high):
    factor_of = 1.0
    for axis_at, blocks in pieces:
        draws = jax.random.uniform(jax.random.fold_in(jax.random.fold_in(rng, 6), axis_at), (blocks,), jnp.float32, low / len(pieces), high / len(pieces))
        factor_of = factor_of * jnp.repeat(jnp.exp(draws), extent[axis_at] // blocks).reshape((-1,) + (1,) * (len(extent) - 1 - axis_at))
    return factor_of


def bell_draw(stream_key, shape, deviation, most, pieces=(), held_as=jnp.bfloat16):
    result = deviation * jax.random.normal(stream_key, shape, jnp.float32)
    if pieces:
        result = result * block_scale(stream_key, shape, pieces, -0.22, 0.18)
    return jnp.clip(result, -most, most).astype(held_as)


def setup_inputs(seed: int = 0) -> dict:
    keys = jax.random.split(jax.random.key(seed), 6)
    gate_pre = bell_draw(keys[0], (TOKENS, FF), 1.0, 6.0, ((0, 16), (1, 16)))
    up_pre = bell_draw(keys[1], (TOKENS, FF), 1.0, 6.0, ((0, 16), (1, 16)))
    grad_out = bell_draw(keys[2], (TOKENS, D), 0.1, 0.59765625, ((0, 256),))
    error = bell_draw(keys[3], (REPLICAS, FF, D), 0.5, 3.0, ((0, 16), (1, 16)))
    sketch = bell_draw(keys[4], (R, D), 1.0, 6.0, (), jnp.float32)
    return {"gate_pre": gate_pre, "up_pre": up_pre, "grad_out": grad_out, "error": error, "sketch": sketch}


def reference(gate_pre, up_pre, grad_out, error, sketch):
    hidden = (jax.nn.silu(gate_pre.astype(jnp.float32)) * up_pre.astype(jnp.float32)).astype(jnp.bfloat16)
    width_dev = FF // N_TENSOR
    hidden_by = jnp.moveaxis(hidden.reshape(N_DP, TOK, N_TENSOR, width_dev), 2, 0)
    error_by = jnp.moveaxis(error.reshape(N_DP, N_TENSOR, width_dev, D), 1, 0)
    grad_rows = grad_out.reshape(N_DP, TOK, D).astype(jnp.float32)
    high = lax.Precision.HIGHEST
    projected = jnp.einsum('itd,rd->itr', grad_rows, sketch, precision=high)
    scale = jnp.sqrt(jnp.float32(width_dev))

    def per_shard(operands):
        hidden_t, error_t = operands
        hidden_f = hidden_t.astype(jnp.float32)
        error_f = error_t.astype(jnp.float32)
        left = jnp.einsum('itf,itr->rf', hidden_f, projected, precision=high)
        left = left + jnp.einsum('ifd,rd->rf', error_f, sketch, precision=high)
        gram = jnp.dot(left, left.T, precision=high)
        chol = jnp.linalg.cholesky(gram)
        ortho = jax.scipy.linalg.solve_triangular(chol, left, lower=True)
        mixed = jnp.einsum('rf,itf->itr', ortho, hidden_f, precision=high)
        right = jnp.einsum('itr,itd->rd', mixed, grad_rows, precision=high)
        right = right + jnp.einsum('rf,ifd->rd', ortho, error_f, precision=high)
        return (ortho * scale, right / (N_DP * scale))
    left_all, right_all = lax.map(per_shard, (hidden_by, error_by))
    p_factor = jnp.moveaxis(left_all, 0, 1).reshape(R, FF)
    return (p_factor, right_all)
```

```python
import functools

import jax
import jax.numpy as jnp
from jax import lax
from jax.experimental import pallas as pl
from jax.experimental.pallas import tpu as pltpu
from jax.sharding import PartitionSpec as P

MESH = pl.DeviceIdType.MESH
HIGH = lax.Precision.HIGHEST
F32 = jnp.float32
BF16 = jnp.bfloat16
NT = (((1,), (1,)), ((), ()))
NN = (((1,), (0,)), ((), ()))

D = 4096
WIDTH = 896
TOK = 1024
R = 32
DP = 16
TENSOR = 16
X = 4
Y = 4
OWN = 64
COLS = D // Y
CH = D // DP
LC = 256


def dot(a, b, dims=NN, precision=None):
    return lax.dot_general(a, b, dims, precision=precision, preferred_element_type=F32)


def split(value):
    high = value.astype(BF16)
    low = (value - high.astype(F32)).astype(BF16)
    return jnp.concatenate([high, low], axis=0)


def fold(product):
    half = product.shape[0] // 2
    return product[:half] + product[half:]


def inverse_factor(gram):
    rows = lax.broadcasted_iota(jnp.int32, (R, 128), 0)
    lanes = lax.broadcasted_iota(jnp.int32, (R, 128), 1)
    wide = jnp.concatenate([gram, jnp.zeros((R, 128 - R), F32)], axis=1)
    wide = jnp.where(lanes == rows + R, 1.0, wide)
    for k in range(R):
        factor = wide[:, k : k + 1] / wide[k : k + 1, k : k + 1]
        wide = wide - jnp.where(rows > k, factor * wide[k : k + 1, :], 0.0)
    pivots = jnp.sum(jnp.where(lanes == rows, wide, 0.0), axis=1, keepdims=True)
    return wide * lax.rsqrt(pivots)


def kernel(
    gate_hbm, up_hbm, g_hbm, e_hbm, sk_hbm,
    p_ref, q_ref,
    gate, up, hidden, g, e, sk, sks, gcols,
    proj, proj_in, proj_all, left, left_in, left_red, left_all, leftw,
    mix, mix_in, inv, inv_in, part, part_in, right, right_in, red, qbuf,
    load_sem,
    proj_s, proj_r, gy_s, gy_r, gx_s, gx_r, ls_s, ls_r, la_s, la_r,
    mx_s, mx_r, iv_s, iv_r, pt_s, pt_r, rs_s, rs_r, ra_s, ra_r,
):
    dp = lax.axis_index("dp")
    tensor = lax.axis_index("tensor")
    mx = tensor // Y
    my = lax.rem(tensor, Y)

    loads = [
        pltpu.make_async_copy(sk_hbm, sk, load_sem.at[0]),
        pltpu.make_async_copy(g_hbm, g, load_sem.at[1]),
        pltpu.make_async_copy(gate_hbm, gate, load_sem.at[2]),
        pltpu.make_async_copy(up_hbm, up, load_sem.at[3]),
        pltpu.make_async_copy(e_hbm, e, load_sem.at[4]),
    ]
    for load in loads:
        load.start()
    own_cols = pltpu.make_async_copy(
        g_hbm.at[:, pl.ds(pl.multiple_of(my * COLS, COLS), COLS)], gcols.at[tensor], load_sem.at[5]
    )
    own_cols.start()

    barrier = pltpu.get_barrier_semaphore()

    @pl.loop(1, TENSOR)
    def _(k):
        pl.semaphore_signal(barrier, inc=1, device_id={"tensor": lax.rem(tensor + k, TENSOR)}, device_id_type=MESH)

    @pl.loop(1, DP)
    def _(k):
        pl.semaphore_signal(barrier, inc=1, device_id={"dp": lax.rem(dp + k, DP)}, device_id_type=MESH)

    def to_tensor(src, dst, send, recv, peer):
        return pltpu.make_async_remote_copy(
            src_ref=src, dst_ref=dst, send_sem=send, recv_sem=recv, device_id={"tensor": peer}, device_id_type=MESH
        )

    def to_dp(src, dst, send, recv, k):
        return pltpu.make_async_remote_copy(
            src_ref=src, dst_ref=dst, send_sem=send, recv_sem=recv,
            device_id={"dp": lax.rem(dp + k, DP)}, device_id_type=MESH,
        )

    def y_peer(k):
        return mx * Y + lax.rem(my + k, Y)

    def x_peer(k):
        return lax.rem(mx + k, X) * Y + my

    def proj_copy(k):
        return to_tensor(proj, proj_in.at[tensor], proj_s.at[k], proj_r.at[k], lax.rem(tensor + k, TENSOR))

    def gy_copy(k):
        there = lax.rem(my + k, Y)
        return to_tensor(
            g.at[:, pl.ds(pl.multiple_of(there * COLS, COLS), COLS)], gcols.at[tensor], gy_s.at[k], gy_r.at[k], y_peer(k)
        )

    def gx_copy(k):
        rows = gcols.at[pl.ds(mx * Y, Y)]
        return to_tensor(rows, rows, gx_s.at[k], gx_r.at[k], x_peer(k))

    def ls_copy(k):
        return to_dp(left.at[lax.rem(dp + k, DP)], left_in.at[k], ls_s.at[k], ls_r.at[k], k)

    def la_copy(k):
        return to_dp(left_red, left_all.at[dp], la_s.at[k], la_r.at[k], k)

    def mix_copy(k):
        return to_tensor(mix, mix_in.at[k], mx_s.at[k], mx_r.at[k], y_peer(k))

    def inv_copy(k):
        return to_tensor(inv, inv_in.at[k], iv_s.at[k], iv_r.at[k], y_peer(k))

    def part_copy(k):
        return to_tensor(part.at[k], part_in.at[k], pt_s.at[k], pt_r.at[k], y_peer(k))

    def rs_copy(k):
        return to_dp(right.at[lax.rem(dp + k, DP)], right_in.at[k], rs_s.at[k], rs_r.at[k], k)

    def ra_copy(k):
        return to_dp(red, qbuf.at[dp], ra_s.at[k], ra_r.at[k], k)

    def start(copy, count):
        pl.loop(1, count)(lambda k: copy(k).start())

    def arrived(copy, count):
        pl.loop(1, count)(lambda k: copy(k).wait_recv())

    def sent(copy, count):
        pl.loop(1, count)(lambda k: copy(k).wait_send())

    loads[0].wait()
    sks[...] = split(sk[...])
    loads[1].wait()
    projected = fold(dot(sks[...], g[...], NT))
    high = projected.astype(BF16)
    low = (projected - high.astype(F32)).astype(BF16)
    proj[...] = jnp.concatenate([high, low], axis=1)
    proj_in[tensor] = proj[...]

    pl.semaphore_wait(barrier, TENSOR - 1 + DP - 1)
    start(proj_copy, TENSOR)
    start(gy_copy, Y)

    loads[2].wait()
    loads[3].wait()

    @pl.loop(0, TOK // 64)
    def _(j):
        rows = pl.ds(pl.multiple_of(j * 64, 64), 64)
        v = gate[rows, :].astype(F32)
        u = up[rows, :].astype(F32)
        hidden[rows, :] = (v / (1.0 + jnp.exp(-v)) * u).astype(BF16)

    arrived(gy_copy, Y)
    own_cols.wait()
    start(gx_copy, X)

    loads[4].wait()
    for j in range(WIDTH // 128):
        leftw[:, j * 128 : (j + 1) * 128] = fold(dot(sks[...], e[j * 128 : (j + 1) * 128, :], NT))

    arrived(proj_copy, TENSOR)
    for j in range(TENSOR // 2):
        a = proj_in[2 * j]
        b = proj_in[2 * j + 1]
        proj_all[0:R, j * 128 : (j + 1) * 128] = jnp.concatenate([a[:, :OWN], b[:, :OWN]], axis=1)
        proj_all[R : 2 * R, j * 128 : (j + 1) * 128] = jnp.concatenate([a[:, OWN:], b[:, OWN:]], axis=1)
    mine = leftw[...] + fold(dot(proj_all[...], hidden[...]))
    mine = jnp.concatenate([mine, jnp.zeros((R, Y * LC - WIDTH), F32)], axis=1)
    for p in range(DP):
        left[p] = mine[8 * (p // 4) : 8 * (p // 4) + 8, LC * (p % 4) : LC * (p % 4) + LC]

    start(ls_copy, DP)
    arrived(ls_copy, DP)
    left_red[...] = left[dp] + functools.reduce(jnp.add, [left_in[k] for k in range(1, DP)])
    left_all[dp] = left_red[...]
    start(la_copy, DP)
    arrived(la_copy, DP)
    for p in range(DP):
        width = min(LC, WIDTH - LC * (p % 4))
        leftw[8 * (p // 4) : 8 * (p // 4) + 8, LC * (p % 4) : LC * (p % 4) + width] = left_all[p][:, :width]

    whole = leftw[...]
    mix[...] = split(fold(dot(split(whole), hidden[...], NT)))
    start(mix_copy, Y)

    factor = inverse_factor(dot(whole, whole, NT, HIGH))
    inv[...] = factor
    start(inv_copy, Y)
    ortho = dot(factor[:, R : 2 * R], whole, NN, HIGH)
    p_ref[...] = ortho * (float(WIDTH) ** 0.5)
    ortho2 = split(ortho)

    @pl.loop(0, DP)
    def _(j):
        right[j] = fold(dot(ortho2, e[:, pl.ds(pl.multiple_of(j * CH, CH), CH)]))

    arrived(gx_copy, X)
    columns = gcols.reshape(TOK, COLS)

    def product(mixed, factor_there, target):
        value = mixed[0:R].astype(F32) + mixed[R : 2 * R].astype(F32)
        value = split(dot(factor_there[:, R : 2 * R], value, NN, HIGH))
        for j in range(Y):
            target(j, fold(dot(value, columns[:, j * CH : (j + 1) * CH])))

    def send_part(k):
        mix_copy(k).wait_recv()
        inv_copy(k).wait_recv()

        def keep(j, block):
            part[lax.rem(Y - k, Y), j] = block

        product(mix_in[k], inv_in[k], keep)
        part_copy(lax.rem(Y - k, Y)).start()

    pl.loop(1, Y)(send_part)

    def add_own(j, block):
        right[my * Y + j] += block

    product(mix[...], factor, add_own)

    @pl.loop(1, Y)
    def _(k):
        part_copy(k).wait_recv()
        there = lax.rem(my + Y - k, Y)
        for j in range(Y):
            right[there * Y + j] += part_in[k, j]

    start(rs_copy, DP)
    arrived(rs_copy, DP)
    total = right[dp] + functools.reduce(jnp.add, [right_in[k] for k in range(1, DP)])
    red[...] = (total * (1.0 / (DP * float(WIDTH) ** 0.5))).astype(BF16)
    qbuf[dp] = red[...]
    start(ra_copy, DP)
    arrived(ra_copy, DP)
    for p in range(DP):
        q_ref[:, p * CH : (p + 1) * CH] = qbuf[p]

    sent(proj_copy, TENSOR)
    sent(gy_copy, Y)
    sent(gx_copy, X)
    sent(ls_copy, DP)
    sent(la_copy, DP)
    sent(mix_copy, Y)
    sent(inv_copy, Y)
    sent(part_copy, Y)
    sent(rs_copy, DP)
    sent(ra_copy, DP)


def shards(gate_pre, up_pre, grad_out, error, sketch):
    vmem = pltpu.VMEM
    dma = pltpu.SemaphoreType.DMA
    scratch = [
        vmem((TOK, WIDTH), BF16),
        vmem((TOK, WIDTH), BF16),
        vmem((TOK, WIDTH), BF16),
        vmem((OWN, D), BF16),
        vmem((WIDTH, D), BF16),
        vmem((R, D), F32),
        vmem((2 * R, D), BF16),
        vmem((TENSOR, OWN, COLS), BF16),
        vmem((R, 2 * OWN), BF16),
        vmem((TENSOR, R, 2 * OWN), BF16),
        vmem((2 * R, TOK), BF16),
        vmem((DP, 8, LC), F32),
        vmem((DP, 8, LC), F32),
        vmem((8, LC), F32),
        vmem((DP, 8, LC), F32),
        vmem((R, WIDTH), F32),
        vmem((2 * R, TOK), BF16),
        vmem((Y, 2 * R, TOK), BF16),
        vmem((R, 128), F32),
        vmem((Y, R, 128), F32),
        vmem((Y, Y, R, CH), F32),
        vmem((Y, Y, R, CH), F32),
        vmem((DP, R, CH), F32),
        vmem((DP, R, CH), F32),
        vmem((R, CH), BF16),
        vmem((DP, R, CH), BF16),
        dma((6,)),
        dma((TENSOR,)), dma((TENSOR,)),
        dma((Y,)), dma((Y,)),
        dma((X,)), dma((X,)),
        dma((DP,)), dma((DP,)),
        dma((DP,)), dma((DP,)),
        dma((Y,)), dma((Y,)),
        dma((Y,)), dma((Y,)),
        dma((Y,)), dma((Y,)),
        dma((DP,)), dma((DP,)),
        dma((DP,)), dma((DP,)),
    ]
    p_factor, q_factor = pl.pallas_call(
        kernel,
        out_shape=(jax.ShapeDtypeStruct((R, WIDTH), F32), jax.ShapeDtypeStruct((R, D), BF16)),
        in_specs=[pl.BlockSpec(memory_space=pl.ANY)] * 5,
        out_specs=(pl.BlockSpec(memory_space=pltpu.VMEM), pl.BlockSpec(memory_space=pltpu.VMEM)),
        scratch_shapes=scratch,
        compiler_params=pltpu.CompilerParams(
            collective_id=0, has_side_effects=True, vmem_limit_bytes=56 * 1024 * 1024
        ),
    )(gate_pre, up_pre, grad_out, error[0], sketch)
    return p_factor, q_factor.astype(F32)[None]


def solution(mesh):
    return jax.shard_map(
        shards,
        mesh=mesh,
        in_specs=(
            P("dp", "tensor"),
            P("dp", "tensor"),
            P(("dp", "tensor"), None),
            P("dp", "tensor", None),
            P(),
        ),
        out_specs=(P(None, "tensor"), P("tensor", None, None)),
        check_vma=False,
    )
```

```python
import functools

import jax
import jax.numpy as jnp
from jax import lax
from jax.experimental import pallas as pl
from jax.experimental.pallas import tpu as pltpu
from jax.sharding import PartitionSpec as P

MESH = pl.DeviceIdType.MESH
HIGH = lax.Precision.HIGHEST
F32 = jnp.float32
BF16 = jnp.bfloat16
NT = (((1,), (1,)), ((), ()))
NN = (((1,), (0,)), ((), ()))

D = 4096
WIDTH = 896
TOK = 1024
R = 32
DP = 16
TENSOR = 16
X = 4
Y = 4
Z = 8
OWN = 64
HALF = D // 2
COLS = HALF // 4
CH = D // DP
LC = 256


def dot(a, b, dims=NN, precision=None):
    return lax.dot_general(a, b, dims, precision=precision, preferred_element_type=F32)


def split(value):
    high = value.astype(BF16)
    low = (value - high.astype(F32)).astype(BF16)
    return jnp.concatenate([high, low], axis=0)


def fold(product):
    half = product.shape[0] // 2
    return product[:half] + product[half:]


def inverse_factor(gram):
    rows = lax.broadcasted_iota(jnp.int32, (R, 128), 0)
    lanes = lax.broadcasted_iota(jnp.int32, (R, 128), 1)
    wide = jnp.concatenate([gram, jnp.zeros((R, 128 - R), F32)], axis=1)
    wide = jnp.where(lanes == rows + R, 1.0, wide)
    for k in range(R):
        factor = wide[:, k : k + 1] / wide[k : k + 1, k : k + 1]
        wide = wide - jnp.where(rows > k, factor * wide[k : k + 1, :], 0.0)
    pivots = jnp.sum(jnp.where(lanes == rows, wide, 0.0), axis=1, keepdims=True)
    return (wide * lax.rsqrt(pivots))[:, R : 2 * R]


def kernel(
    gate_hbm, up_hbm, g_hbm, e_hbm, sk_hbm,
    p_ref, q_ref,
    gate, up, hidden, g, e, sk, sks, gcols,
    proj, proj_in, proj_all, left, left_in, left_red, left_all, leftw,
    mix, errors, errors_in, part, part_in, psum, swap_in, right, right_in, red, qbuf,
    load_sem,
    proj_s, proj_r, gs_s, gs_r, gl_s, gl_r, ls_s, ls_r, la_s, la_r,
    mx_s, mx_r, ec_s, ec_r, pc_s, pc_r, sw_s, sw_r, rs_s, rs_r, ra_s, ra_r, fw_s, fw_r,
):
    dp = lax.axis_index("dp")
    tensor = lax.axis_index("tensor")
    mx = tensor // Y
    my = lax.rem(tensor, Y)
    mz = dp // 2
    core = lax.rem(dp, 2)

    barrier = pltpu.get_barrier_semaphore()

    @pl.loop(1, TENSOR)
    def _(k):
        pl.semaphore_signal(barrier, inc=1, device_id={"tensor": lax.rem(tensor + k, TENSOR)}, device_id_type=MESH)

    @pl.loop(1, DP)
    def _(k):
        pl.semaphore_signal(barrier, inc=1, device_id={"dp": lax.rem(dp + k, DP)}, device_id_type=MESH)

    def cols(half, place):
        return pl.ds(pl.multiple_of(half * HALF + place * COLS, COLS), COLS)

    loads = [
        pltpu.make_async_copy(sk_hbm, sk, load_sem.at[0]),
        pltpu.make_async_copy(g_hbm, g, load_sem.at[1]),
        pltpu.make_async_copy(gate_hbm, gate, load_sem.at[2]),
        pltpu.make_async_copy(up_hbm, up, load_sem.at[3]),
        pltpu.make_async_copy(e_hbm, e, load_sem.at[4]),
        pltpu.make_async_copy(g_hbm.at[:, cols(0, my)], gcols.at[0, tensor], load_sem.at[5]),
        pltpu.make_async_copy(g_hbm.at[:, cols(1, mx)], gcols.at[1, tensor], load_sem.at[6]),
    ]
    for load in loads:
        load.start()

    def remote(src, dst, send, recv, peer):
        return pltpu.make_async_remote_copy(
            src_ref=src, dst_ref=dst, send_sem=send, recv_sem=recv, device_id=peer, device_id_type=MESH
        )

    def y_peer(k):
        return {"tensor": mx * Y + lax.rem(my + k, Y)}

    def x_peer(k):
        return {"tensor": lax.rem(mx + k, X) * Y + my}

    def dp_peer(k):
        return {"dp": lax.rem(dp + k, DP)}

    def z_peer(k):
        return {"dp": lax.rem(mz + k, Z) * 2 + core}

    other_core = {"dp": mz * 2 + 1 - core}

    def proj_copy(k):
        return remote(
            proj, proj_in.at[tensor], proj_s.at[k], proj_r.at[k], {"tensor": lax.rem(tensor + k, TENSOR)}
        )

    def ga_copy(k):
        return remote(
            g.at[:, cols(0, lax.rem(my + k, Y))], gcols.at[0, tensor], gs_s.at[0, k], gs_r.at[0, k], y_peer(k)
        )

    def gb_copy(k):
        return remote(
            g.at[:, cols(1, lax.rem(mx + k, X))], gcols.at[1, tensor], gs_s.at[1, k], gs_r.at[1, k], x_peer(k)
        )

    def gax_copy(k):
        rows = gcols.at[0, pl.ds(mx * Y, Y)]
        return remote(rows, rows, gl_s.at[0, k], gl_r.at[0, k], x_peer(k))

    def gby_copy(i, k):
        row = gcols.at[1, i * Y + my]
        return remote(row, row, gl_s.at[1 + i, k], gl_r.at[1 + i, k], y_peer(k))

    def ls_copy(k):
        return remote(left.at[lax.rem(dp + k, DP)], left_in.at[k], ls_s.at[k], ls_r.at[k], dp_peer(k))

    def la_copy(k):
        return remote(left_red, left_all.at[dp], la_s.at[k], la_r.at[k], dp_peer(k))

    def mixa_copy(k):
        return remote(mix.at[0, 0], mix.at[0, k], mx_s.at[0, k], mx_r.at[0, k], y_peer(k))

    def mixb_copy(k):
        return remote(mix.at[0, 0], mix.at[1, k], mx_s.at[1, k], mx_r.at[1, k], x_peer(k))

    errors_copy = remote(errors.at[1 - core], errors_in, ec_s.at[0], ec_r.at[0], other_core)

    def part_copy(half):
        return remote(part.at[1 - core, half], part_in.at[half], pc_s.at[half], pc_r.at[half], other_core)

    def swapa_copy(k):
        return remote(psum.at[0, k], swap_in.at[0, k], sw_s.at[0, k], sw_r.at[0, k], y_peer(k))

    def swapb_copy(k):
        return remote(psum.at[1, k], swap_in.at[1, k], sw_s.at[1, k], sw_r.at[1, k], x_peer(k))

    def rs_copy(k):
        return remote(right.at[lax.rem(mz + k, Z)], right_in.at[k], rs_s.at[k], rs_r.at[k], z_peer(k))

    def ra_copy(k):
        return remote(red, qbuf.at[dp], ra_s.at[k], ra_r.at[k], z_peer(k))

    def fw_copy(k):
        chunk = qbuf.at[lax.rem(mz + Z - k, Z) * 2 + core]
        return remote(chunk, chunk, fw_s.at[k], fw_r.at[k], other_core)

    def start(copy, count):
        pl.loop(1, count)(lambda k: copy(k).start())

    def arrived(copy, count):
        pl.loop(1, count)(lambda k: copy(k).wait_recv())

    def sent(copy, count):
        pl.loop(1, count)(lambda k: copy(k).wait_send())

    loads[0].wait()
    sks[...] = split(sk[...])
    loads[1].wait()
    projected = fold(dot(sks[...], g[...], NT))
    high = projected.astype(BF16)
    low = (projected - high.astype(F32)).astype(BF16)
    proj[...] = jnp.concatenate([high, low], axis=1)
    proj_in[tensor] = proj[...]

    pl.semaphore_wait(barrier, TENSOR - 1 + DP - 1)
    start(proj_copy, TENSOR)
    start(ga_copy, Y)
    start(gb_copy, X)

    loads[2].wait()
    loads[3].wait()

    @pl.loop(0, TOK // 64)
    def _(j):
        rows = pl.ds(pl.multiple_of(j * 64, 64), 64)
        v = gate[rows, :].astype(F32)
        u = up[rows, :].astype(F32)
        hidden[rows, :] = (v / (1.0 + jnp.exp(-v)) * u).astype(BF16)

    loads[4].wait()
    for at in range(0, WIDTH, 256):
        to = min(at + 256, WIDTH)
        leftw[:, at:to] = fold(dot(sks[...], e[at:to, :], NT))

    arrived(proj_copy, TENSOR)
    for j in range(TENSOR // 2):
        a = proj_in[2 * j]
        b = proj_in[2 * j + 1]
        proj_all[0:R, j * 128 : (j + 1) * 128] = jnp.concatenate([a[:, :OWN], b[:, :OWN]], axis=1)
        proj_all[R : 2 * R, j * 128 : (j + 1) * 128] = jnp.concatenate([a[:, OWN:], b[:, OWN:]], axis=1)
    mine = leftw[...] + fold(dot(proj_all[...], hidden[...]))
    mine = jnp.concatenate([mine, jnp.zeros((R, 4 * LC - WIDTH), F32)], axis=1)
    for p in range(DP):
        left[p] = mine[8 * (p // 4) : 8 * (p // 4) + 8, LC * (p % 4) : LC * (p % 4) + LC]

    start(ls_copy, DP)
    loads[5].wait()
    loads[6].wait()
    arrived(ga_copy, Y)
    start(gax_copy, X)
    arrived(gb_copy, X)

    @pl.loop(0, X)
    def _(i):
        start(functools.partial(gby_copy, i), Y)

    arrived(ls_copy, DP)
    left_red[...] = left[dp] + functools.reduce(jnp.add, [left_in[k] for k in range(1, DP)])
    left_all[dp] = left_red[...]
    start(la_copy, DP)
    arrived(la_copy, DP)
    for p in range(DP):
        width = min(LC, WIDTH - LC * (p % 4))
        leftw[8 * (p // 4) : 8 * (p // 4) + 8, LC * (p % 4) : LC * (p % 4) + width] = left_all[p][:, :width]

    whole = split(leftw[...])
    mixed = split(fold(dot(whole, hidden[...], NT)))
    mix[0, 0] = mixed
    start(mixa_copy, Y)
    start(mixb_copy, X)
    mix[1, 0] = mixed

    @pl.loop(0, Z)
    def _(j):
        for half in range(2):
            at = pl.multiple_of(j * 2 * CH + half * CH, CH)
            errors[half, j] = fold(dot(whole, e[:, pl.ds(at, CH)]))

    errors_copy.start()

    arrived(gax_copy, X)

    def product(side):
        rows = mix[side].reshape(4 * 2 * R, TOK)
        for half in range(2):
            block = dot(rows, gcols[side, :, :, half * CH : (half + 1) * CH].reshape(TOK, CH))
            for k in range(4):
                part[half, side, (4 - k) % 4] = fold(block[2 * R * k : 2 * R * (k + 1)])

    arrived(mixa_copy, Y)
    product(0)
    part_copy(0).start()

    @pl.loop(0, X)
    def _(i):
        arrived(functools.partial(gby_copy, i), Y)

    arrived(mixb_copy, X)
    product(1)
    part_copy(1).start()

    errors_copy.wait_recv()
    for j in range(Z):
        right[j] = errors[core, j] + errors_in[j]
    for side, copy in ((0, swapa_copy), (1, swapb_copy)):
        part_copy(side).wait_recv()
        for k in range(4):
            psum[side, k] = part[core, side, k] + part_in[side, k]
        start(copy, 4)
    right[my] += psum[0, 0]
    right[4 + mx] += psum[1, 0]

    @pl.loop(1, 4)
    def _(k):
        swapa_copy(k).wait_recv()
        right[lax.rem(my + 4 - k, 4)] += swap_in[0, k]

    @pl.loop(1, 4)
    def _(k):
        swapb_copy(k).wait_recv()
        right[4 + lax.rem(mx + 4 - k, 4)] += swap_in[1, k]

    start(rs_copy, Z)

    full = leftw[...]
    factor = inverse_factor(dot(full, full, NT, HIGH))
    p_ref[...] = dot(factor, full, NN, HIGH) * (float(WIDTH) ** 0.5)
    sent(proj_copy, TENSOR)
    sent(ga_copy, Y)
    sent(gb_copy, X)
    sent(gax_copy, X)

    @pl.loop(0, X)
    def _(i):
        sent(functools.partial(gby_copy, i), Y)

    sent(ls_copy, DP)
    sent(la_copy, DP)
    sent(mixa_copy, Y)
    sent(mixb_copy, X)
    errors_copy.wait_send()
    part_copy(0).wait_send()
    part_copy(1).wait_send()
    sent(swapa_copy, Y)
    sent(swapb_copy, X)

    arrived(rs_copy, Z)
    total = right[mz] + functools.reduce(jnp.add, [right_in[k] for k in range(1, Z)])
    total = dot(factor, total, NN, HIGH) * (1.0 / (DP * float(WIDTH) ** 0.5))
    red[...] = total.astype(BF16)
    start(ra_copy, Z)
    qbuf[dp] = red[...]
    fw_copy(0).start()

    @pl.loop(1, Z)
    def _(k):
        ra_copy(k).wait_recv()
        fw_copy(k).start()

    pl.loop(0, Z)(lambda k: fw_copy(k).wait_recv())
    for p in range(DP):
        q_ref[:, p * CH : (p + 1) * CH] = qbuf[p]

    sent(rs_copy, Z)
    sent(ra_copy, Z)
    pl.loop(0, Z)(lambda k: fw_copy(k).wait_send())


def finish(p_in, q_in, p_out, q_out):
    p_out[...] = p_in[...]
    q_out[0] = q_in[...].astype(F32)


def shards(gate_pre, up_pre, grad_out, error, sketch):
    vmem = pltpu.VMEM
    dma = pltpu.SemaphoreType.DMA
    scratch = [
        vmem((TOK, WIDTH), BF16),
        vmem((TOK, WIDTH), BF16),
        vmem((TOK, WIDTH), BF16),
        vmem((OWN, D), BF16),
        vmem((WIDTH, D), BF16),
        vmem((R, D), F32),
        vmem((2 * R, D), BF16),
        vmem((2, TENSOR, OWN, COLS), BF16),
        vmem((R, 2 * OWN), BF16),
        vmem((TENSOR, R, 2 * OWN), BF16),
        vmem((2 * R, TOK), BF16),
        vmem((DP, 8, LC), F32),
        vmem((DP, 8, LC), F32),
        vmem((8, LC), F32),
        vmem((DP, 8, LC), F32),
        vmem((R, WIDTH), F32),
        vmem((2, 4, 2 * R, TOK), BF16),
        vmem((2, Z, R, CH), F32),
        vmem((Z, R, CH), F32),
        vmem((2, 2, 4, R, CH), F32),
        vmem((2, 4, R, CH), F32),
        vmem((2, 4, R, CH), F32),
        vmem((2, 4, R, CH), F32),
        vmem((Z, R, CH), F32),
        vmem((Z, R, CH), F32),
        vmem((R, CH), BF16),
        vmem((DP, R, CH), BF16),
        dma((7,)),
        dma((TENSOR,)), dma((TENSOR,)),
        dma((2, 4)), dma((2, 4)),
        dma((5, 4)), dma((5, 4)),
        dma((DP,)), dma((DP,)),
        dma((DP,)), dma((DP,)),
        dma((2, 4)), dma((2, 4)),
        dma((1,)), dma((1,)),
        dma((2,)), dma((2,)),
        dma((2, 4)), dma((2, 4)),
        dma((Z,)), dma((Z,)),
        dma((Z,)), dma((Z,)),
        dma((Z,)), dma((Z,)),
    ]
    p_factor, q_factor = pl.pallas_call(
        kernel,
        out_shape=(jax.ShapeDtypeStruct((R, WIDTH), F32), jax.ShapeDtypeStruct((R, D), BF16)),
        in_specs=[pl.BlockSpec(memory_space=pl.ANY)] * 5,
        out_specs=(pl.BlockSpec(memory_space=pltpu.VMEM), pl.BlockSpec(memory_space=pltpu.VMEM)),
        scratch_shapes=scratch,
        compiler_params=pltpu.CompilerParams(
            collective_id=0, has_side_effects=True, vmem_limit_bytes=56 * 1024 * 1024
        ),
    )(gate_pre, up_pre, grad_out, error[0], sketch)
    return pl.pallas_call(
        finish,
        out_shape=(jax.ShapeDtypeStruct((R, WIDTH), F32), jax.ShapeDtypeStruct((1, R, D), F32)),
    )(p_factor, q_factor)


def solution(mesh):
    return jax.shard_map(
        shards,
        mesh=mesh,
        in_specs=(
            P("dp", "tensor"),
            P("dp", "tensor"),
            P(("dp", "tensor"), None),
            P("dp", "tensor", None),
            P(),
        ),
        out_specs=(P(None, "tensor"), P("tensor", None, None)),
        check_vma=False,
    )
```

```python
import functools

import jax
import jax.numpy as jnp
from jax import lax
from jax.experimental import pallas as pl
from jax.experimental.pallas import tpu as pltpu
from jax.sharding import PartitionSpec as P

MESH = pl.DeviceIdType.MESH
HIGH = lax.Precision.HIGHEST
F32 = jnp.float32
BF16 = jnp.bfloat16
NT = (((1,), (1,)), ((), ()))
NN = (((1,), (0,)), ((), ()))

D = 4096
WIDTH = 896
TOK = 1024
R = 32
DP = 16
TENSOR = 16
X = 4
Y = 4
Z = 8
OWN = 64
HALF = D // 2
COLS = HALF // 4
CH = D // DP
LC = 256


def dot(a, b, dims=NN, precision=None):
    return lax.dot_general(a, b, dims, precision=precision, preferred_element_type=F32)


def split(value):
    high = value.astype(BF16)
    low = (value - high.astype(F32)).astype(BF16)
    return jnp.concatenate([high, low], axis=0)


def fold(product):
    half = product.shape[0] // 2
    return product[:half] + product[half:]


def inverse_factor(gram):
    rows = lax.broadcasted_iota(jnp.int32, (R, 128), 0)
    lanes = lax.broadcasted_iota(jnp.int32, (R, 128), 1)
    wide = jnp.concatenate([gram, jnp.zeros((R, 128 - R), F32)], axis=1)
    wide = jnp.where(lanes == rows + R, 1.0, wide)
    for k in range(R):
        factor = wide[:, k : k + 1] / wide[k : k + 1, k : k + 1]
        wide = wide - jnp.where(rows > k, factor * wide[k : k + 1, :], 0.0)
    pivots = jnp.sum(jnp.where(lanes == rows, wide, 0.0), axis=1, keepdims=True)
    return (wide * lax.rsqrt(pivots))[:, R : 2 * R]


def kernel(
    gate_hbm, up_hbm, g_hbm, e_hbm, sk_hbm,
    p_ref, q_ref,
    gate, up, hidden, g, e, sk, sks, gcols,
    proj, proj_in, proj_all, left, left_half, left_in, left_red, left_all, leftw,
    mix, errors, errors_in, esum, esum_in, part, part_in, psum, psum_in, red, qbuf,
    load_sem,
    proj_s, proj_r, gs_s, gs_r, gl_s, gl_r, lc_s, lc_r, ls_s, ls_r, la_s, la_r, lf_s, lf_r,
    mx_s, mx_r, ec_s, ec_r, es_s, es_r, pc_s, pc_r, ps_s, ps_r, ra_s, ra_r, fw_s, fw_r,
):
    dp = lax.axis_index("dp")
    tensor = lax.axis_index("tensor")
    mx = tensor // Y
    my = lax.rem(tensor, Y)
    mz = dp // 2
    core = lax.rem(dp, 2)

    def cols(half, place):
        return pl.ds(pl.multiple_of(half * HALF + place * COLS, COLS), COLS)

    loads = [
        pltpu.make_async_copy(sk_hbm, sk, load_sem.at[0]),
        pltpu.make_async_copy(g_hbm, g, load_sem.at[1]),
        pltpu.make_async_copy(gate_hbm, gate, load_sem.at[2]),
        pltpu.make_async_copy(up_hbm, up, load_sem.at[3]),
        pltpu.make_async_copy(e_hbm, e, load_sem.at[4]),
        pltpu.make_async_copy(g_hbm.at[:, cols(0, my)], gcols.at[0, tensor], load_sem.at[5]),
        pltpu.make_async_copy(g_hbm.at[:, cols(1, mx)], gcols.at[1, tensor], load_sem.at[6]),
    ]
    for load in loads:
        load.start()

    barrier = pltpu.get_barrier_semaphore()

    @pl.loop(1, TENSOR)
    def _(k):
        pl.semaphore_signal(barrier, inc=1, device_id={"tensor": lax.rem(tensor + k, TENSOR)}, device_id_type=MESH)

    @pl.loop(1, DP)
    def _(k):
        pl.semaphore_signal(barrier, inc=1, device_id={"dp": lax.rem(dp + k, DP)}, device_id_type=MESH)

    block_y = lax.rem(my + Y - lax.rem(mz, Y), Y)
    block_x = lax.rem(mx + X - lax.rem(mz, X), X)
    source = jnp.where(mz < Y, mx * Y + block_y, block_x * Y + my)
    own_source = lax.rem(mz, Y) == 0

    @pl.loop(0, Z)
    def _(z):
        @pl.when(jnp.logical_not(jnp.logical_and(own_source, z == mz)))
        def _():
            pl.semaphore_signal(
                barrier, inc=1, device_id={"dp": z * 2 + core, "tensor": source}, device_id_type=MESH
            )

    def remote(src, dst, send, recv, peer):
        return pltpu.make_async_remote_copy(
            src_ref=src, dst_ref=dst, send_sem=send, recv_sem=recv, device_id=peer, device_id_type=MESH
        )

    def y_peer(k):
        return {"tensor": mx * Y + lax.rem(my + k, Y)}

    def x_peer(k):
        return {"tensor": lax.rem(mx + k, X) * Y + my}

    def dp_peer(k):
        return {"dp": lax.rem(dp + k, DP)}

    def z_peer(k):
        return {"dp": lax.rem(mz + k, Z) * 2 + core}

    other_core = {"dp": mz * 2 + 1 - core}

    def proj_copy(k):
        return remote(
            proj, proj_in.at[tensor], proj_s.at[0], proj_r.at[0], {"tensor": lax.rem(tensor + k, TENSOR)}
        )

    def ga_copy(k):
        return remote(
            g.at[:, cols(0, lax.rem(my + k, Y))], gcols.at[0, tensor], gs_s.at[0], gs_r.at[0, k], y_peer(k)
        )

    def gb_copy(k):
        return remote(
            g.at[:, cols(1, lax.rem(mx + k, X))], gcols.at[1, tensor], gs_s.at[1], gs_r.at[1, k], x_peer(k)
        )

    def gax_copy(i, k):
        row = gcols.at[0, mx * Y + i]
        return remote(row, row, gl_s.at[0], gl_r.at[0], x_peer(k))

    def gby_copy(i, k):
        row = gcols.at[1, i * Y + my]
        return remote(row, row, gl_s.at[1], gl_r.at[1], y_peer(k))

    def lc_copy():
        rows = left.at[pl.ds((1 - core) * Z, Z)]
        return remote(rows, left_half, lc_s.at[0], lc_r.at[0], other_core)

    def ls_copy(k):
        return remote(left.at[core * Z + lax.rem(mz + k, Z)], left_in.at[k], ls_s.at[0], ls_r.at[0], z_peer(k))

    def la_copy(k):
        return remote(left_red, left_all.at[core * Z + mz], la_s.at[0], la_r.at[k], z_peer(k))

    def lf_copy(k):
        held = left_all.at[core * Z + lax.rem(mz + Z - k, Z)]
        return remote(held, held, lf_s.at[0], lf_r.at[0], other_core)

    def mixa_copy(k):
        return remote(mix.at[0, 0], mix.at[0, k], mx_s.at[0], mx_r.at[0], y_peer(k))

    def mixb_copy(k):
        return remote(mix.at[0, 0], mix.at[1, k], mx_s.at[1], mx_r.at[1], x_peer(k))

    errors_copy = remote(errors.at[1 - core], errors_in, ec_s.at[0], ec_r.at[0], other_core)

    def part_copy(half):
        return remote(part.at[1 - core, half], part_in.at[half], pc_s.at[half], pc_r.at[half], other_core)

    def chunk(z):
        return jnp.where(z < Y, lax.rem(my + Y - lax.rem(z, Y), Y), Y + lax.rem(mx + X - lax.rem(z, X), X))

    def es_copy(k):
        return remote(esum.at[chunk(lax.rem(mz + k, Z))], esum_in.at[k], es_s.at[0], es_r.at[0], z_peer(k))

    def psa_copy(k):
        peer = {"dp": k * 2 + core, "tensor": mx * Y + lax.rem(my + k, Y)}
        return remote(psum.at[0, k], psum_in.at[mz], ps_s.at[0], ps_r.at[0], peer)

    def psb_copy(k):
        peer = {"dp": (Y + k) * 2 + core, "tensor": lax.rem(mx + k, X) * Y + my}
        return remote(psum.at[1, k], psum_in.at[mz], ps_s.at[1], ps_r.at[0], peer)

    def ra_copy(k):
        return remote(red, qbuf.at[chunk(mz) * 2 + core], ra_s.at[0], ra_r.at[k], z_peer(k))

    def fw_copy(k):
        held = qbuf.at[chunk(lax.rem(mz + Z - k, Z)) * 2 + core]
        return remote(held, held, fw_s.at[0], fw_r.at[0], other_core)

    def start(copy, count):
        pl.loop(1, count)(lambda k: copy(k).start())

    def took(like, sem):
        pltpu.make_async_copy(like, like, sem).wait()

    loads[0].wait()
    sks[...] = split(sk[...])
    loads[1].wait()
    projected = fold(dot(sks[...], g[...], NT))
    high = projected.astype(BF16)
    low = (projected - high.astype(F32)).astype(BF16)
    proj[...] = jnp.concatenate([high, low], axis=1)
    proj_in[tensor] = proj[...]

    pl.semaphore_wait(barrier, TENSOR - 1 + DP - 1 + Z - own_source.astype(jnp.int32))
    start(proj_copy, TENSOR)
    start(ga_copy, Y)
    start(gb_copy, X)

    loads[5].wait()
    loads[6].wait()
    start(functools.partial(gax_copy, my), X)
    start(functools.partial(gby_copy, mx), Y)

    loads[2].wait()
    loads[3].wait()

    @pl.loop(0, TOK // 64)
    def _(j):
        rows = pl.ds(pl.multiple_of(j * 64, 64), 64)
        v = gate[rows, :].astype(F32)
        u = up[rows, :].astype(F32)
        hidden[rows, :] = (v / (1.0 + jnp.exp(-v)) * u).astype(BF16)

    loads[4].wait()
    for at in range(0, WIDTH, 256):
        to = min(at + 256, WIDTH)
        leftw[:, at:to] = fold(dot(sks[...], e[at:to, :], NT))

    took(proj_in.at[pl.ds(1, TENSOR - 1)], proj_r.at[0])
    for j in range(TENSOR // 2):
        a = proj_in[2 * j]
        b = proj_in[2 * j + 1]
        proj_all[0:R, j * 128 : (j + 1) * 128] = jnp.concatenate([a[:, :OWN], b[:, :OWN]], axis=1)
        proj_all[R : 2 * R, j * 128 : (j + 1) * 128] = jnp.concatenate([a[:, OWN:], b[:, OWN:]], axis=1)
    mine = leftw[...] + fold(dot(proj_all[...], hidden[...]))
    mine = jnp.concatenate([mine, jnp.zeros((R, 4 * LC - WIDTH), F32)], axis=1)
    for p in range(DP):
        left[p] = mine[8 * (p // 4) : 8 * (p // 4) + 8, LC * (p % 4) : LC * (p % 4) + LC]

    lc_copy().start()
    lc_copy().wait_recv()
    for j in range(Z):
        left[core * Z + j] += left_half[j]
    start(ls_copy, Z)
    @pl.loop(1, 4)
    def _(k):
        ga_copy(k).wait_recv()
        start(functools.partial(gax_copy, lax.rem(my + Y - k, Y)), X)
        gb_copy(k).wait_recv()
        start(functools.partial(gby_copy, lax.rem(mx + X - k, X)), Y)

    took(left_in.at[pl.ds(1, Z - 1)], ls_r.at[0])
    left_red[...] = left[core * Z + mz] + functools.reduce(jnp.add, [left_in[k] for k in range(1, Z)])
    start(la_copy, Z)
    left_all[core * Z + mz] = left_red[...]
    lf_copy(0).start()

    @pl.loop(1, Z)
    def _(k):
        la_copy(k).wait_recv()
        lf_copy(k).start()

    took(left_all.at[pl.ds(0, Z)], lf_r.at[0])
    for p in range(DP):
        width = min(LC, WIDTH - LC * (p % 4))
        leftw[8 * (p // 4) : 8 * (p // 4) + 8, LC * (p % 4) : LC * (p % 4) + width] = left_all[p][:, :width]

    whole = split(leftw[...])
    mixed = split(fold(dot(whole, hidden[...], NT)))
    mix[0, 0] = mixed
    start(mixa_copy, Y)
    start(mixb_copy, X)
    mix[1, 0] = mixed

    @pl.loop(0, Z)
    def _(j):
        for half in range(2):
            at = pl.multiple_of(j * 2 * CH + half * CH, CH)
            errors[half, j] = fold(dot(whole, e[:, pl.ds(at, CH)]))

    errors_copy.start()
    errors_copy.wait_recv()
    for j in range(Z):
        esum[j] = errors[core, j] + errors_in[j]
    start(es_copy, Z)

    took(gcols.at[0, pl.ds(0, 12)], gl_r.at[0])

    def product(side):
        rows = mix[side].reshape(4 * 2 * R, TOK)
        for half in range(2):
            block = dot(rows, gcols[side, :, :, half * CH : (half + 1) * CH].reshape(TOK, CH))
            for k in range(4):
                part[half, side, (4 - k) % 4] = fold(block[2 * R * k : 2 * R * (k + 1)])

    took(mix.at[0, pl.ds(1, 3)], mx_r.at[0])
    product(0)
    part_copy(0).start()
    took(gcols.at[1, pl.ds(0, 12)], gl_r.at[1])
    took(mix.at[1, pl.ds(1, 3)], mx_r.at[1])
    product(1)
    part_copy(1).start()

    def pieces(side, copy):
        part_copy(side).wait_recv()
        for k in range(4):
            psum[side, k] = part[core, side, k] + part_in[side, k]
        start(copy, 4)

        @pl.when(mz == 4 * side)
        def _():
            pltpu.make_async_copy(psum.at[side, 0], psum_in.at[mz], ps_r.at[0]).start()

        @pl.when(mz != 4 * side)
        def _():
            copy(0).start()

    pieces(0, psa_copy)
    pieces(1, psb_copy)

    full = leftw[...]
    factor = inverse_factor(dot(full, full, NT, HIGH))
    p_ref[...] = dot(factor, full, NN, HIGH) * (float(WIDTH) ** 0.5)
    took(proj_in.at[pl.ds(1, TENSOR - 1)], proj_s.at[0])
    for side in range(2):
        took(gcols.at[side, pl.ds(0, 3)], gs_s.at[side])
        took(gcols.at[side, pl.ds(0, 12)], gl_s.at[side])
        took(mix.at[side, pl.ds(1, 3)], mx_s.at[side])
        part_copy(side).wait_send()
    lc_copy().wait_send()
    took(left_in.at[pl.ds(1, Z - 1)], ls_s.at[0])
    took(left_in.at[pl.ds(1, Z - 1)], la_s.at[0])
    took(left_in, lf_s.at[0])
    errors_copy.wait_send()
    took(esum_in.at[pl.ds(1, Z - 1)], es_s.at[0])

    took(esum_in.at[pl.ds(1, Z - 1)], es_r.at[0])
    total = esum[chunk(mz)] + functools.reduce(jnp.add, [esum_in[k] for k in range(1, Z)])
    took(psum_in, ps_r.at[0])
    total = total + functools.reduce(jnp.add, [psum_in[z] for z in range(Z)])
    total = dot(factor, total, NN, HIGH) * (1.0 / (DP * float(WIDTH) ** 0.5))
    red[...] = total.astype(BF16)
    start(ra_copy, Z)
    qbuf[chunk(mz) * 2 + core] = red[...]
    fw_copy(0).start()

    @pl.loop(1, Z)
    def _(k):
        ra_copy(k).wait_recv()
        fw_copy(k).start()

    took(qbuf.at[pl.ds(0, Z)], fw_r.at[0])
    for p in range(DP):
        q_ref[:, p * CH : (p + 1) * CH] = qbuf[p].astype(F32)

    for side in range(2):
        took(psum.at[side, pl.ds(0, 3)], ps_s.at[side])

        @pl.when(mz != 4 * side)
        def _():
            took(psum.at[side, 0], ps_s.at[side])

    took(qbuf.at[pl.ds(0, Z - 1)], ra_s.at[0])
    took(qbuf.at[pl.ds(0, Z)], fw_s.at[0])


def shards(gate_pre, up_pre, grad_out, error, sketch):
    vmem = pltpu.VMEM
    dma = pltpu.SemaphoreType.DMA
    scratch = [
        vmem((TOK, WIDTH), BF16),
        vmem((TOK, WIDTH), BF16),
        vmem((TOK, WIDTH), BF16),
        vmem((OWN, D), BF16),
        vmem((WIDTH, D), BF16),
        vmem((R, D), F32),
        vmem((2 * R, D), BF16),
        vmem((2, TENSOR, OWN, COLS), BF16),
        vmem((R, 2 * OWN), BF16),
        vmem((TENSOR, R, 2 * OWN), BF16),
        vmem((2 * R, TOK), BF16),
        vmem((DP, 8, LC), F32),
        vmem((Z, 8, LC), F32),
        vmem((Z, 8, LC), F32),
        vmem((8, LC), F32),
        vmem((DP, 8, LC), F32),
        vmem((R, WIDTH), F32),
        vmem((2, 4, 2 * R, TOK), BF16),
        vmem((2, Z, R, CH), F32),
        vmem((Z, R, CH), F32),
        vmem((Z, R, CH), F32),
        vmem((Z, R, CH), F32),
        vmem((2, 2, 4, R, CH), F32),
        vmem((2, 4, R, CH), F32),
        vmem((2, 4, R, CH), F32),
        vmem((Z, R, CH), F32),
        vmem((R, CH), BF16),
        vmem((DP, R, CH), BF16),
        dma((7,)),
        dma((1,)), dma((1,)),
        dma((2,)), dma((2, 4)),
        dma((2,)), dma((2,)),
        dma((1,)), dma((1,)),
        dma((1,)), dma((1,)),
        dma((1,)), dma((Z,)),
        dma((1,)), dma((1,)),
        dma((2,)), dma((2,)),
        dma((1,)), dma((1,)),
        dma((1,)), dma((1,)),
        dma((2,)), dma((2,)),
        dma((2,)), dma((1,)),
        dma((1,)), dma((Z,)),
        dma((1,)), dma((1,)),
    ]
    p_factor, q_factor = pl.pallas_call(
        kernel,
        out_shape=(pltpu.VMEM((R, WIDTH), F32), pltpu.VMEM((R, D), F32)),
        in_specs=[pl.BlockSpec(memory_space=pl.ANY)] * 5,
        out_specs=(pl.BlockSpec(memory_space=pltpu.VMEM), pl.BlockSpec(memory_space=pltpu.VMEM)),
        scratch_shapes=scratch,
        compiler_params=pltpu.CompilerParams(
            collective_id=0, has_side_effects=True, vmem_limit_bytes=56 * 1024 * 1024
        ),
    )(gate_pre, up_pre, grad_out, error[0], sketch)
    return p_factor, q_factor[None]


def solution(mesh):
    return jax.shard_map(
        shards,
        mesh=mesh,
        in_specs=(
            P("dp", "tensor"),
            P("dp", "tensor"),
            P(("dp", "tensor"), None),
            P("dp", "tensor", None),
            P(),
        ),
        out_specs=(P(None, "tensor"), P("tensor", None, None)),
        check_vma=False,
    )
```

```python
import functools

import jax
import jax.numpy as jnp
from jax import lax
from jax.experimental import pallas as pl
from jax.experimental.pallas import tpu as pltpu
from jax.sharding import PartitionSpec as P

MESH = pl.DeviceIdType.MESH
HIGH = lax.Precision.HIGHEST
F32 = jnp.float32
BF16 = jnp.bfloat16
NT = (((1,), (1,)), ((), ()))
NN = (((1,), (0,)), ((), ()))

D = 4096
WIDTH = 896
TOK = 1024
R = 32
PARTS = 4
RH = R // PARTS
DP = 16
TENSOR = 16
X = 4
Y = 4
Z = 8
OWN = 64
HALF = D // 2
COLS = HALF // 4
CH = D // DP
LC = 256
RING4 = (2, 1, 3)
RING8 = (4, 3, 5, 2, 6, 1, 7)
GRID = tuple(
    sorted(
        ((a, b) for a in range(X) for b in range(Y) if a or b),
        key=lambda k: -min(k[0], X - k[0]) - min(k[1], Y - k[1]),
    )
)
LAG = 4


def dot(a, b, dims=NN, precision=None):
    return lax.dot_general(a, b, dims, precision=precision, preferred_element_type=F32)


def split(value):
    high = value.astype(BF16)
    low = (value - high.astype(F32)).astype(BF16)
    return jnp.concatenate([high, low], axis=0)


def fold(product):
    half = product.shape[0] // 2
    return product[:half] + product[half:]


def inverse_factor(gram):
    rows = lax.broadcasted_iota(jnp.int32, (R, 128), 0)
    lanes = lax.broadcasted_iota(jnp.int32, (R, 128), 1)
    wide = jnp.concatenate([gram, jnp.zeros((R, 128 - R), F32)], axis=1)
    wide = jnp.where(lanes == rows + R, 1.0, wide)
    for k in range(R):
        factor = wide[:, k : k + 1] / wide[k : k + 1, k : k + 1]
        wide = wide - jnp.where(rows > k, factor * wide[k : k + 1, :], 0.0)
    pivots = jnp.sum(jnp.where(lanes == rows, wide, 0.0), axis=1, keepdims=True)
    return (wide * lax.rsqrt(pivots))[:, R : 2 * R]


def kernel(
    gate_hbm, up_hbm, g_hbm, e_hbm, sk_hbm,
    p_ref, q_ref,
    gate, up, hidden, g, e, sk, sks, gcols,
    proj, proj_in, proj_all, left, left_half, left_in, left_red, left_all, leftw,
    mix, errors, errors_in, esum, esum_in, part, part_in, psum, psum_in, red, qbuf,
    load_sem,
    proj_s, proj_r, gs_s, gs_r, gl_s, gl_r, lc_s, lc_r, ls_s, ls_r, la_s, la_r, lf_s, lf_r,
    mx_s, mx_r, ec_s, ec_r, es_s, es_r, pc_s, pc_r, ps_s, ps_r, ra_s, ra_r, fw_s, fw_r,
):
    dp = lax.axis_index("dp")
    tensor = lax.axis_index("tensor")
    mx = tensor // Y
    my = lax.rem(tensor, Y)
    mz = dp // 2
    core = lax.rem(dp, 2)

    def cols(half, place):
        return pl.ds(pl.multiple_of(half * HALF + place * COLS, COLS), COLS)

    loads = [
        pltpu.make_async_copy(sk_hbm, sk, load_sem.at[0]),
        pltpu.make_async_copy(g_hbm, g, load_sem.at[1]),
        pltpu.make_async_copy(gate_hbm, gate, load_sem.at[2]),
        pltpu.make_async_copy(up_hbm, up, load_sem.at[3]),
        pltpu.make_async_copy(e_hbm, e, load_sem.at[4]),
        pltpu.make_async_copy(g_hbm.at[:, cols(0, my)], gcols.at[0, tensor], load_sem.at[5]),
        pltpu.make_async_copy(g_hbm.at[:, cols(1, mx)], gcols.at[1, tensor], load_sem.at[6]),
    ]
    for load in loads:
        load.start()

    barrier = pltpu.get_barrier_semaphore()

    @pl.loop(1, TENSOR)
    def _(k):
        pl.semaphore_signal(barrier, inc=1, device_id={"tensor": lax.rem(tensor + k, TENSOR)}, device_id_type=MESH)

    @pl.loop(1, DP)
    def _(k):
        pl.semaphore_signal(barrier, inc=1, device_id={"dp": lax.rem(dp + k, DP)}, device_id_type=MESH)

    block_y = lax.rem(my + Y - lax.rem(mz, Y), Y)
    block_x = lax.rem(mx + X - lax.rem(mz, X), X)
    source = jnp.where(mz < Y, mx * Y + block_y, block_x * Y + my)
    own_source = lax.rem(mz, Y) == 0

    @pl.loop(0, Z)
    def _(z):
        @pl.when(jnp.logical_not(jnp.logical_and(own_source, z == mz)))
        def _():
            pl.semaphore_signal(
                barrier, inc=1, device_id={"dp": z * 2 + core, "tensor": source}, device_id_type=MESH
            )

    def remote(src, dst, send, recv, peer):
        return pltpu.make_async_remote_copy(
            src_ref=src, dst_ref=dst, send_sem=send, recv_sem=recv, device_id=peer, device_id_type=MESH
        )

    def y_peer(k):
        return {"tensor": mx * Y + lax.rem(my + k, Y)}

    def x_peer(k):
        return {"tensor": lax.rem(mx + k, X) * Y + my}

    def dp_peer(k):
        return {"dp": lax.rem(dp + k, DP)}

    def z_peer(k):
        return {"dp": lax.rem(mz + k, Z) * 2 + core}

    other_core = {"dp": mz * 2 + 1 - core}

    def proj_copy(k):
        return remote(
            proj, proj_in.at[tensor], proj_s.at[0], proj_r.at[0],
            {"tensor": lax.rem(mx + k[0], X) * Y + lax.rem(my + k[1], Y)},
        )

    def ga_copy(k):
        return remote(
            g.at[:, cols(0, lax.rem(my + k, Y))], gcols.at[0, tensor], gs_s.at[0], gs_r.at[0, k], y_peer(k)
        )

    def gb_copy(k):
        return remote(
            g.at[:, cols(1, lax.rem(mx + k, X))], gcols.at[1, tensor], gs_s.at[1], gs_r.at[1, k], x_peer(k)
        )

    def gax_copy(i, k):
        row = gcols.at[0, mx * Y + i]
        return remote(row, row, gl_s.at[0], gl_r.at[0], x_peer(k))

    def gby_copy(i, k):
        row = gcols.at[1, i * Y + my]
        return remote(row, row, gl_s.at[1], gl_r.at[1], y_peer(k))

    def lc_copy():
        rows = left.at[pl.ds((1 - core) * Z, Z)]
        return remote(rows, left_half, lc_s.at[0], lc_r.at[0], other_core)

    def ls_copy(k):
        return remote(left.at[core * Z + lax.rem(mz + k, Z)], left_in.at[k], ls_s.at[0], ls_r.at[0], z_peer(k))

    def la_copy(k):
        return remote(left_red, left_all.at[core * Z + mz], la_s.at[0], la_r.at[k], z_peer(k))

    def lf_copy(k):
        held = left_all.at[core * Z + lax.rem(mz + Z - k, Z)]
        return remote(held, held, lf_s.at[0], lf_r.at[0], other_core)

    def mix_copy(half, side, k):
        return remote(
            mix.at[half, 0, 0], mix.at[half, side, k], mx_s.at[half, side], mx_r.at[half, side],
            (y_peer, x_peer)[side](k),
        )

    def errors_copy(j):
        return remote(errors.at[1 - core, j], errors_in.at[j], ec_s.at[0], ec_r.at[j], other_core)

    def chunk(z):
        return jnp.where(z < Y, lax.rem(my + Y - lax.rem(z, Y), Y), Y + lax.rem(mx + X - lax.rem(z, X), X))

    def owner(j):
        return jnp.where(j < Y, lax.rem(my + Y - lax.rem(j, Y), Y), Y + lax.rem(mx + X - lax.rem(j, X), X))

    def es_copy(j):
        return remote(esum.at[j], esum_in.at[mz], es_s.at[0], es_r.at[0], {"dp": owner(j) * 2 + core})

    def part_copy(half, side):
        return remote(
            part.at[half, 1 - core, side], part_in.at[half, side], pc_s.at[half, side], pc_r.at[half, side], other_core
        )

    def ps_copy(half, side, k):
        there = (mx * Y + lax.rem(my + k, Y), lax.rem(mx + k, X) * Y + my)[side]
        return remote(
            psum.at[half, side, k], psum_in.at[half, mz], ps_s.at[half, side], ps_r.at[half],
            {"dp": (Y * side + k) * 2 + core, "tensor": there},
        )

    def ra_copy(k):
        return remote(red, qbuf.at[chunk(mz) * 2 + core], ra_s.at[0], ra_r.at[k], z_peer(k))

    def fw_copy(k):
        held = qbuf.at[chunk(lax.rem(mz + Z - k, Z)) * 2 + core]
        return remote(held, held, fw_s.at[0], fw_r.at[0], other_core)

    def start(copy, order):
        for k in order:
            copy(k).start()

    def took(like, sem):
        pltpu.make_async_copy(like, like, sem).wait()

    loads[0].wait()
    sks[...] = split(sk[...])
    loads[1].wait()
    projected = fold(dot(sks[...], g[...], NT))
    high = projected.astype(BF16)
    low = (projected - high.astype(F32)).astype(BF16)
    proj[...] = jnp.concatenate([high, low], axis=1)
    proj_in[tensor] = proj[...]

    pl.semaphore_wait(barrier, TENSOR - 1 + DP - 1 + Z - own_source.astype(jnp.int32))
    start(proj_copy, GRID)
    start(ga_copy, RING4)
    start(gb_copy, RING4)

    loads[5].wait()
    loads[6].wait()
    start(functools.partial(gax_copy, my), RING4)
    start(functools.partial(gby_copy, mx), RING4)

    loads[2].wait()
    loads[3].wait()

    @pl.loop(0, TOK // 64)
    def _(j):
        rows = pl.ds(pl.multiple_of(j * 64, 64), 64)
        v = gate[rows, :].astype(F32)
        u = up[rows, :].astype(F32)
        hidden[rows, :] = (v / (1.0 + jnp.exp(-v)) * u).astype(BF16)

    loads[4].wait()
    for at in range(0, WIDTH, 256):
        to = min(at + 256, WIDTH)
        leftw[:, at:to] = fold(dot(sks[...], e[at:to, :], NT))

    took(proj_in.at[pl.ds(1, TENSOR - 1)], proj_r.at[0])
    for j in range(TENSOR // 2):
        a = proj_in[2 * j]
        b = proj_in[2 * j + 1]
        proj_all[0:R, j * 128 : (j + 1) * 128] = jnp.concatenate([a[:, :OWN], b[:, :OWN]], axis=1)
        proj_all[R : 2 * R, j * 128 : (j + 1) * 128] = jnp.concatenate([a[:, OWN:], b[:, OWN:]], axis=1)
    mine = leftw[...] + fold(dot(proj_all[...], hidden[...]))
    mine = jnp.concatenate([mine, jnp.zeros((R, 4 * LC - WIDTH), F32)], axis=1)
    for p in range(DP):
        left[p] = mine[8 * (p // 4) : 8 * (p // 4) + 8, LC * (p % 4) : LC * (p % 4) + LC]

    lc_copy().start()
    lc_copy().wait_recv()
    for j in range(Z):
        left[core * Z + j] += left_half[j]
    start(ls_copy, RING8)
    @pl.loop(1, 4)
    def _(k):
        ga_copy(k).wait_recv()
        start(functools.partial(gax_copy, lax.rem(my + Y - k, Y)), RING4)
        gb_copy(k).wait_recv()
        start(functools.partial(gby_copy, lax.rem(mx + X - k, X)), RING4)

    took(left_in.at[pl.ds(1, Z - 1)], ls_r.at[0])
    left_red[...] = left[core * Z + mz] + functools.reduce(jnp.add, [left_in[k] for k in range(1, Z)])
    start(la_copy, RING8)
    left_all[core * Z + mz] = left_red[...]
    lf_copy(0).start()

    for k in reversed(RING8):
        la_copy(k).wait_recv()
        lf_copy(k).start()

    took(left_all.at[pl.ds(0, Z)], lf_r.at[0])
    for p in range(DP):
        width = min(LC, WIDTH - LC * (p % 4))
        leftw[8 * (p // 4) : 8 * (p // 4) + 8, LC * (p % 4) : LC * (p % 4) + width] = left_all[p][:, :width]

    whole = split(leftw[...])
    mixed = fold(dot(whole, hidden[...], NT))
    for half in range(PARTS):
        mix[half, 0, 0] = split(mixed[RH * half : RH * (half + 1)])
        for side in range(2):
            start(functools.partial(mix_copy, half, side), RING4)
    for half in range(PARTS):
        mix[half, 1, 0] = mix[half, 0, 0]

    @pl.loop(0, Z + LAG)
    def _(j):
        @pl.when(j < Z)
        def _():
            for part_of in range(2):
                at = pl.multiple_of(j * 2 * CH + part_of * CH, CH)
                errors[part_of, j] = fold(dot(whole, e[:, pl.ds(at, CH)]))
            errors_copy(j).start()

        @pl.when(j >= LAG)
        def _():
            i = j - LAG
            errors_copy(i).wait_recv()
            esum[i] = errors[core, i] + errors_in[i]

            @pl.when(owner(i) == mz)
            def _():
                esum_in[mz] = esum[i]

            @pl.when(owner(i) != mz)
            def _():
                es_copy(i).start()

    def product(half, side):
        took(mix.at[half, side, pl.ds(1, 3)], mx_r.at[half, side])
        rows = mix[half, side].reshape(4 * 2 * RH, TOK)
        for part_of in range(2):
            block = dot(rows, gcols[side, :, :, part_of * CH : (part_of + 1) * CH].reshape(TOK, CH))
            for k in range(4):
                part[half, part_of, side, (4 - k) % 4] = fold(block[2 * RH * k : 2 * RH * (k + 1)])
        part_copy(half, side).start()

    def pieces(half, side):
        part_copy(half, side).wait_recv()
        for k in range(4):
            psum[half, side, k] = part[half, core, side, k] + part_in[half, side, k]
        start(functools.partial(ps_copy, half, side), RING4)

        @pl.when(mz == 4 * side)
        def _():
            pltpu.make_async_copy(psum.at[half, side, 0], psum_in.at[half, mz], ps_r.at[half]).start()

        @pl.when(mz != 4 * side)
        def _():
            ps_copy(half, side, 0).start()

    for side in range(2):
        took(gcols.at[side, pl.ds(0, 12)], gl_r.at[side])
    for half in range(PARTS):
        for side in range(2):
            product(half, side)
        for side in range(2):
            pieces(half, side)

    full = leftw[...]
    factor = inverse_factor(dot(full, full, NT, HIGH))
    p_ref[...] = dot(factor, full, NN, HIGH) * (float(WIDTH) ** 0.5)
    took(proj_in.at[pl.ds(1, TENSOR - 1)], proj_s.at[0])
    for side in range(2):
        took(gcols.at[side, pl.ds(0, 3)], gs_s.at[side])
        took(gcols.at[side, pl.ds(0, 12)], gl_s.at[side])
        for half in range(PARTS):
            took(mix.at[half, side, pl.ds(1, 3)], mx_s.at[half, side])
            part_copy(half, side).wait_send()
    lc_copy().wait_send()
    took(left_in.at[pl.ds(1, Z - 1)], ls_s.at[0])
    took(left_in.at[pl.ds(1, Z - 1)], la_s.at[0])
    took(left_in, lf_s.at[0])
    took(errors_in, ec_s.at[0])
    took(esum_in.at[pl.ds(1, Z - 1)], es_s.at[0])

    took(esum_in.at[pl.ds(1, Z - 1)], es_r.at[0])
    total = functools.reduce(jnp.add, [esum_in[z] for z in range(Z)])
    for half in range(PARTS):
        took(psum_in.at[half], ps_r.at[half])
    total = total + jnp.concatenate(
        [functools.reduce(jnp.add, [psum_in[half, z] for z in range(Z)]) for half in range(PARTS)], axis=0
    )
    total = dot(factor, total, NN, HIGH) * (1.0 / (DP * float(WIDTH) ** 0.5))
    red[...] = total.astype(BF16)
    start(ra_copy, RING8)
    qbuf[chunk(mz) * 2 + core] = red[...]
    fw_copy(0).start()

    for k in reversed(RING8):
        ra_copy(k).wait_recv()
        fw_copy(k).start()

    took(qbuf.at[pl.ds(0, Z)], fw_r.at[0])
    for p in range(DP):
        q_ref[:, p * CH : (p + 1) * CH] = qbuf[p].astype(F32)

    for half in range(PARTS):
        for side in range(2):
            took(psum.at[half, side, pl.ds(0, 3)], ps_s.at[half, side])

            @pl.when(mz != 4 * side)
            def _():
                took(psum.at[half, side, 0], ps_s.at[half, side])

    took(qbuf.at[pl.ds(0, Z - 1)], ra_s.at[0])
    took(qbuf.at[pl.ds(0, Z)], fw_s.at[0])


def finish(p_in, q_in, p_out, q_out, sem):
    copies = [pltpu.make_async_copy(p_in, p_out, sem.at[0]), pltpu.make_async_copy(q_in, q_out.at[0], sem.at[1])]
    for copy in copies:
        copy.start()
    for copy in copies:
        copy.wait()


def shards(gate_pre, up_pre, grad_out, error, sketch):
    vmem = pltpu.VMEM
    dma = pltpu.SemaphoreType.DMA
    scratch = [
        vmem((TOK, WIDTH), BF16),
        vmem((TOK, WIDTH), BF16),
        vmem((TOK, WIDTH), BF16),
        vmem((OWN, D), BF16),
        vmem((WIDTH, D), BF16),
        vmem((R, D), F32),
        vmem((2 * R, D), BF16),
        vmem((2, TENSOR, OWN, COLS), BF16),
        vmem((R, 2 * OWN), BF16),
        vmem((TENSOR, R, 2 * OWN), BF16),
        vmem((2 * R, TOK), BF16),
        vmem((DP, 8, LC), F32),
        vmem((Z, 8, LC), F32),
        vmem((Z, 8, LC), F32),
        vmem((8, LC), F32),
        vmem((DP, 8, LC), F32),
        vmem((R, WIDTH), F32),
        vmem((PARTS, 2, 4, 2 * RH, TOK), BF16),
        vmem((2, Z, R, CH), F32),
        vmem((Z, R, CH), F32),
        vmem((Z, R, CH), F32),
        vmem((Z, R, CH), F32),
        vmem((PARTS, 2, 2, 4, RH, CH), F32),
        vmem((PARTS, 2, 4, RH, CH), F32),
        vmem((PARTS, 2, 4, RH, CH), F32),
        vmem((PARTS, Z, RH, CH), F32),
        vmem((R, CH), BF16),
        vmem((DP, R, CH), BF16),
        dma((7,)),
        dma((1,)), dma((1,)),
        dma((2,)), dma((2, 4)),
        dma((2,)), dma((2,)),
        dma((1,)), dma((1,)),
        dma((1,)), dma((1,)),
        dma((1,)), dma((Z,)),
        dma((1,)), dma((1,)),
        dma((PARTS, 2)), dma((PARTS, 2)),
        dma((1,)), dma((Z,)),
        dma((1,)), dma((1,)),
        dma((PARTS, 2)), dma((PARTS, 2)),
        dma((PARTS, 2)), dma((PARTS,)),
        dma((1,)), dma((Z,)),
        dma((1,)), dma((1,)),
    ]
    p_factor, q_factor = pl.pallas_call(
        kernel,
        out_shape=(pltpu.VMEM((R, WIDTH), F32), pltpu.VMEM((R, D), F32)),
        in_specs=[pl.BlockSpec(memory_space=pl.ANY)] * 5,
        out_specs=(pl.BlockSpec(memory_space=pltpu.VMEM), pl.BlockSpec(memory_space=pltpu.VMEM)),
        scratch_shapes=scratch,
        compiler_params=pltpu.CompilerParams(
            collective_id=0, has_side_effects=True, vmem_limit_bytes=56 * 1024 * 1024
        ),
    )(gate_pre, up_pre, grad_out, error[0], sketch)
    return pl.pallas_call(
        finish,
        out_shape=(jax.ShapeDtypeStruct((R, WIDTH), F32), jax.ShapeDtypeStruct((1, R, D), F32)),
        in_specs=[pl.BlockSpec(memory_space=pltpu.VMEM)] * 2,
        out_specs=(pl.BlockSpec(memory_space=pl.ANY), pl.BlockSpec(memory_space=pl.ANY)),
        scratch_shapes=[dma((2,))],
    )(pltpu.with_memory_space_constraint(p_factor, pltpu.VMEM), pltpu.with_memory_space_constraint(q_factor, pltpu.VMEM))


def solution(mesh):
    return jax.shard_map(
        shards,
        mesh=mesh,
        in_specs=(
            P("dp", "tensor"),
            P("dp", "tensor"),
            P(("dp", "tensor"), None),
            P("dp", "tensor", None),
            P(),
        ),
        out_specs=(P(None, "tensor"), P("tensor", None, None)),
        check_vma=False,
    )
```

```python
import functools

import jax
import jax.numpy as jnp
from jax import lax
from jax.experimental import pallas as pl
from jax.experimental.pallas import tpu as pltpu
from jax.sharding import PartitionSpec as P

MESH = pl.DeviceIdType.MESH
HIGH = lax.Precision.HIGHEST
F32 = jnp.float32
BF16 = jnp.bfloat16
NT = (((1,), (1,)), ((), ()))
NN = (((1,), (0,)), ((), ()))

D = 4096
WIDTH = 896
TOK = 1024
R = 32
PARTS = 4
RH = R // PARTS
DP = 16
TENSOR = 16
X = 4
Y = 4
Z = 8
OWN = 64
HALF = D // 2
COLS = HALF // 4
CH = D // DP
LC = 256
RING4 = (2, 1, 3)
RING8 = (4, 3, 5, 2, 6, 1, 7)
GRID = tuple(
    sorted(
        ((a, b) for a in range(X) for b in range(Y) if a or b),
        key=lambda k: -min(k[0], X - k[0]) - min(k[1], Y - k[1]),
    )
)
LAG = 2


def dot(a, b, dims=NN, precision=None):
    return lax.dot_general(a, b, dims, precision=precision, preferred_element_type=F32)


def split(value):
    high = value.astype(BF16)
    low = (value - high.astype(F32)).astype(BF16)
    return jnp.concatenate([high, low], axis=0)


def fold(product):
    half = product.shape[0] // 2
    return product[:half] + product[half:]


def inverse_factor(gram):
    rows = lax.broadcasted_iota(jnp.int32, (R, 128), 0)
    lanes = lax.broadcasted_iota(jnp.int32, (R, 128), 1)
    wide = jnp.concatenate([gram, jnp.zeros((R, 128 - R), F32)], axis=1)
    wide = jnp.where(lanes == rows + R, 1.0, wide)
    for k in range(R):
        factor = wide[:, k : k + 1] / wide[k : k + 1, k : k + 1]
        wide = wide - jnp.where(rows > k, factor * wide[k : k + 1, :], 0.0)
    pivots = jnp.sum(jnp.where(lanes == rows, wide, 0.0), axis=1, keepdims=True)
    return (wide * lax.rsqrt(pivots))[:, R : 2 * R]


def kernel(
    gate_hbm, up_hbm, g_hbm, e_hbm, sk_hbm,
    p_ref, q_ref,
    gate, up, hidden, g, e, sk, sks, gcols,
    proj, proj_in, proj_all, left, left_half, left_in, left_red, left_all, leftw,
    mix, errors, errors_in, esum, esum_in, part, part_in, psum, psum_in, red, qbuf,
    load_sem,
    proj_s, proj_r, gs_s, gs_r, gl_s, gl_r, lc_s, lc_r, ls_s, ls_r, la_s, la_r, lf_s, lf_r,
    mx_s, mx_r, ec_s, ec_r, es_s, es_r, pc_s, pc_r, ps_s, ps_r, ra_s, ra_r, fw_s, fw_r,
):
    dp = lax.axis_index("dp")
    tensor = lax.axis_index("tensor")
    mx = tensor // Y
    my = lax.rem(tensor, Y)
    mz = dp // 2
    core = lax.rem(dp, 2)

    barrier = pltpu.get_barrier_semaphore()

    def signal(peer):
        pl.semaphore_signal(barrier, inc=1, device_id=peer, device_id_type=MESH)

    for a, b in GRID:
        signal({"tensor": lax.rem(mx + a, X) * Y + lax.rem(my + b, Y)})

    def cols(half, place):
        return pl.ds(pl.multiple_of(half * HALF + place * COLS, COLS), COLS)

    loads = [
        pltpu.make_async_copy(sk_hbm, sk, load_sem.at[0]),
        pltpu.make_async_copy(g_hbm, g, load_sem.at[1]),
        pltpu.make_async_copy(gate_hbm, gate, load_sem.at[2]),
        pltpu.make_async_copy(up_hbm, up, load_sem.at[3]),
        pltpu.make_async_copy(e_hbm, e, load_sem.at[4]),
    ]
    for load in loads:
        load.start()

    for k in RING8:
        for other in (core, 1 - core):
            signal({"dp": lax.rem(mz + k, Z) * 2 + other})
    signal({"dp": mz * 2 + 1 - core})

    block_y = lax.rem(my + Y - lax.rem(mz, Y), Y)
    block_x = lax.rem(mx + X - lax.rem(mz, X), X)
    source = jnp.where(mz < Y, mx * Y + block_y, block_x * Y + my)
    own_source = lax.rem(mz, Y) == 0
    for k in RING8:
        signal({"dp": lax.rem(mz + k, Z) * 2 + core, "tensor": source})

    @pl.when(jnp.logical_not(own_source))
    def _():
        signal({"dp": dp, "tensor": source})

    def remote(src, dst, send, recv, peer):
        return pltpu.make_async_remote_copy(
            src_ref=src, dst_ref=dst, send_sem=send, recv_sem=recv, device_id=peer, device_id_type=MESH
        )

    def y_peer(k):
        return {"tensor": mx * Y + lax.rem(my + k, Y)}

    def x_peer(k):
        return {"tensor": lax.rem(mx + k, X) * Y + my}

    def dp_peer(k):
        return {"dp": lax.rem(dp + k, DP)}

    def z_peer(k):
        return {"dp": lax.rem(mz + k, Z) * 2 + core}

    other_core = {"dp": mz * 2 + 1 - core}

    def proj_copy(k):
        return remote(
            proj, proj_in.at[tensor], proj_s.at[0], proj_r.at[0],
            {"tensor": lax.rem(mx + k[0], X) * Y + lax.rem(my + k[1], Y)},
        )

    def ga_copy(k):
        return remote(
            g.at[:, cols(0, lax.rem(my + k, Y))], gcols.at[0, tensor], gs_s.at[0], gs_r.at[0], y_peer(k)
        )

    def gb_copy(k):
        return remote(
            g.at[:, cols(1, lax.rem(mx + k, X))], gcols.at[1, tensor], gs_s.at[0], gs_r.at[1], x_peer(k)
        )

    def gax_copy(i, k):
        row = gcols.at[0, mx * Y + i]
        return remote(row, row, gl_s.at[0], gl_r.at[0], x_peer(k))

    def gby_copy(i, k):
        row = gcols.at[1, i * Y + my]
        return remote(row, row, gl_s.at[0], gl_r.at[1], y_peer(k))

    def own_a():
        return g.at[:, cols(0, my)], gcols.at[0, tensor]

    def own_b():
        return g.at[:, cols(1, mx)], gcols.at[1, tensor]

    def oax_copy(k):
        return remote(*own_a(), gl_s.at[0], gl_r.at[0], x_peer(k))

    def oby_copy(k):
        return remote(*own_b(), gl_s.at[0], gl_r.at[1], y_peer(k))

    def lc_copy():
        rows = left.at[pl.ds((1 - core) * Z, Z)]
        return remote(rows, left_half, lc_s.at[0], lc_r.at[0], other_core)

    def ls_copy(k):
        return remote(left.at[core * Z + lax.rem(mz + k, Z)], left_in.at[k], ls_s.at[0], ls_r.at[0], z_peer(k))

    def la_copy(k):
        return remote(left_red, left_all.at[core * Z + mz], la_s.at[0], la_r.at[min(k, Z - k) - 1], z_peer(k))

    def lf_copy(k):
        held = left_all.at[core * Z + lax.rem(mz + Z - k, Z)]
        return remote(held, held, lf_s.at[0], lf_r.at[0], other_core)

    def mix_copy(half, side, k):
        return remote(
            mix.at[half, 0, 0], mix.at[half, side, k], mx_s.at[0], mx_r.at[half],
            (y_peer, x_peer)[side](k),
        )

    def errors_copy(j):
        pair = pl.ds(2 * j, 2)
        return remote(errors.at[1 - core, pair], errors_in.at[pair], ec_s.at[0], ec_r.at[j], other_core)

    def chunk(z):
        return jnp.where(z < Y, lax.rem(my + Y - lax.rem(z, Y), Y), Y + lax.rem(mx + X - lax.rem(z, X), X))

    def es_copy(n, z):
        return remote(esum.at[n], esum_in.at[mz], es_s.at[0], es_r.at[0], {"dp": z * 2 + core})

    def part_copy(half):
        return remote(part.at[half, 1 - core], part_in.at[half], pc_s.at[0], pc_r.at[half], other_core)

    def ps_copy(half, z):
        k = lax.rem(z, 4)
        there = jnp.where(z < 4, mx * Y + lax.rem(my + k, Y), lax.rem(mx + k, X) * Y + my)
        return remote(
            psum.at[half, z], psum_in.at[half, mz], ps_s.at[0], ps_r.at[0], {"dp": z * 2 + core, "tensor": there}
        )

    def ra_copy(k):
        return remote(red, qbuf.at[chunk(mz) * 2 + core], ra_s.at[0], ra_r.at[min(k, Z - k) - 1], z_peer(k))

    def fw_copy(k):
        held = qbuf.at[chunk(lax.rem(mz + Z - k, Z)) * 2 + core]
        return remote(held, held, fw_s.at[0], fw_r.at[0], other_core)

    def start(copy, order):
        for k in order:
            copy(k).start()

    def took(like, sem):
        pltpu.make_async_copy(like, like, sem).wait()

    loads[0].wait()
    sks[...] = split(sk[...])
    loads[1].wait()
    projected = fold(dot(sks[...], g[...], NT))
    high = projected.astype(BF16)
    low = (projected - high.astype(F32)).astype(BF16)
    proj[...] = jnp.concatenate([high, low], axis=1)
    proj_in[tensor] = proj[...]

    pl.semaphore_wait(barrier, TENSOR - 1 + DP - 1 + Z - own_source.astype(jnp.int32))
    start(proj_copy, GRID)
    start(ga_copy, RING4)
    start(gb_copy, RING4)

    start(oax_copy, RING4)
    start(oby_copy, RING4)
    pltpu.make_async_copy(*own_a(), gl_r.at[0]).start()
    pltpu.make_async_copy(*own_b(), gl_r.at[1]).start()

    loads[2].wait()
    loads[3].wait()

    @pl.loop(0, TOK // 64)
    def _(j):
        rows = pl.ds(pl.multiple_of(j * 64, 64), 64)
        v = gate[rows, :].astype(F32)
        u = up[rows, :].astype(F32)
        hidden[rows, :WIDTH] = (v / (1.0 + jnp.exp(-v)) * u).astype(BF16)
        hidden[rows, WIDTH:] = jnp.zeros((64, 4 * LC - WIDTH), BF16)

    loads[4].wait()
    for at in range(0, WIDTH, 256):
        to = min(at + 256, WIDTH)
        leftw[:, at:to] = fold(dot(sks[...], e[at:to, :], NT))

    took(proj_in.at[pl.ds(1, TENSOR - 1)], proj_r.at[0])
    for j in range(TENSOR // 2):
        a = proj_in[2 * j]
        b = proj_in[2 * j + 1]
        proj_all[0:R, j * 128 : (j + 1) * 128] = jnp.concatenate([a[:, :OWN], b[:, :OWN]], axis=1)
        proj_all[R : 2 * R, j * 128 : (j + 1) * 128] = jnp.concatenate([a[:, OWN:], b[:, OWN:]], axis=1)
    mine = leftw[:, :WIDTH] + fold(dot(proj_all[...], hidden[:, :WIDTH]))
    mine = jnp.concatenate([mine, jnp.zeros((R, 4 * LC - WIDTH), F32)], axis=1)
    for p in range(DP):
        row, at = 8 * (p % Z // 2), 2 * LC * (p // Z) + LC * (p % 2)
        left[p] = mine[row : row + 8, at : at + LC]

    lc_copy().start()
    lc_copy().wait_recv()
    for j in range(Z):
        left[core * Z + j] += left_half[j]
    start(ls_copy, RING8)
    took(gcols.at[0, pl.ds(0, 3)], gs_r.at[0])
    for k in range(1, 4):
        start(functools.partial(gax_copy, lax.rem(my + Y - k, Y)), RING4)
    took(gcols.at[1, pl.ds(0, 3)], gs_r.at[1])
    for k in range(1, 4):
        start(functools.partial(gby_copy, lax.rem(mx + X - k, X)), RING4)

    took(left_in.at[pl.ds(1, Z - 1)], ls_r.at[0])
    left_red[...] = left[core * Z + mz] + functools.reduce(jnp.add, [left_in[k] for k in range(1, Z)])
    start(la_copy, RING8)
    left_all[core * Z + mz] = left_red[...]
    lf_copy(0).start()

    for near in range(1, 5):
        pair = sorted({near, Z - near})
        took(left_all.at[pl.ds(0, len(pair))], la_r.at[near - 1])
        for k in pair:
            lf_copy(k).start()

    def product_of(which):
        chunks = [left_all[which * Z + z] for z in range(Z)]
        value = jnp.concatenate(
            [jnp.concatenate(chunks[2 * i : 2 * i + 2], axis=1) for i in range(Z // 2)], axis=0
        )
        place = pl.ds(pl.multiple_of(which * 2 * LC, 2 * LC), 2 * LC)
        leftw[:, place] = value
        return fold(dot(split(value), hidden[:, place], NT))

    mixed = product_of(core)
    took(left_all.at[pl.ds(0, Z)], lf_r.at[0])
    mixed = mixed + product_of(1 - core)
    for half in range(PARTS):
        mix[half, 0, 0] = split(mixed[RH * half : RH * (half + 1)])
        for side in range(2):
            start(functools.partial(mix_copy, half, side), RING4)
    for half in range(PARTS):
        mix[half, 1, 0] = mix[half, 0, 0]

    whole = split(leftw[:, :WIDTH])

    @pl.loop(0, Z // 2 + LAG)
    def _(j):
        @pl.when(j < Z // 2)
        def _():
            for i, offset in enumerate((4 + j, 3 - j)):
                place = chunk(lax.rem(mz + offset, Z))
                for part_of in range(2):
                    at = pl.multiple_of((2 * place + part_of) * CH, CH)
                    errors[part_of, 2 * j + i] = fold(dot(whole, e[:, pl.ds(at, CH)]))
            errors_copy(j).start()

        @pl.when(j >= LAG)
        def _():
            errors_copy(j - LAG).wait_recv()
            for i, offset in enumerate((4 + (j - LAG), 3 - (j - LAG))):
                n = 2 * (j - LAG) + i
                esum[n] = errors[core, n] + errors_in[n]

                @pl.when(offset == 0)
                def _():
                    esum_in[mz] = esum[n]

                @pl.when(offset != 0)
                def _():
                    es_copy(n, lax.rem(mz + offset, Z)).start()

    gcols_like = gcols.reshape(2 * TENSOR, OWN, COLS)
    mix_like = mix.reshape(PARTS * 2 * 4, 2 * RH, TOK)

    def product(half, side):
        rows = mix[half, side].reshape(4 * 2 * RH, TOK)
        for part_of in range(2):
            block = dot(rows, gcols[side, :, :, part_of * CH : (part_of + 1) * CH].reshape(TOK, CH))
            for k in range(4):
                part[half, part_of, side, (4 - k) % 4] = fold(block[2 * RH * k : 2 * RH * (k + 1)])

    def pieces(half):
        for side in range(2):
            for k in range(4):
                psum[half, 4 * side + k] = part[half, core, side, k] + part_in[half, side, k]
        for offset in RING8:
            ps_copy(half, lax.rem(mz + offset, Z)).start()

        @pl.when(own_source)
        def _():
            pltpu.make_async_copy(psum.at[half, mz], psum_in.at[half, mz], ps_r.at[0]).start()

        @pl.when(jnp.logical_not(own_source))
        def _():
            ps_copy(half, mz).start()

    for side in range(2):
        took(gcols.at[side, pl.ds(0, 13)], gl_r.at[side])
    for half in range(PARTS + 1):
        if half < PARTS:
            took(mix_like.at[pl.ds(0, 6)], mx_r.at[half])
            for side in range(2):
                product(half, side)
            part_copy(half).start()
        if half > 0:
            part_copy(half - 1).wait_recv()
            pieces(half - 1)

    full = leftw[:, :WIDTH]
    factor = inverse_factor(dot(full, full, NT, HIGH))
    p_ref[...] = dot(factor, full, NN, HIGH) * (float(WIDTH) ** 0.5)
    took(proj_in.at[pl.ds(1, TENSOR - 1)], proj_s.at[0])
    took(gcols_like.at[pl.ds(0, 6)], gs_s.at[0])
    took(gcols_like.at[pl.ds(0, 24)], gl_s.at[0])
    took(mix_like.at[pl.ds(0, 6 * PARTS)], mx_s.at[0])
    lc_copy().wait_send()
    took(left_in.at[pl.ds(1, Z - 1)], ls_s.at[0])
    took(left_in.at[pl.ds(1, Z - 1)], la_s.at[0])
    took(left_in, lf_s.at[0])
    took(errors_in, ec_s.at[0])
    took(esum_in.at[pl.ds(1, Z - 1)], es_s.at[0])
    took(part_in, pc_s.at[0])

    took(esum_in.at[pl.ds(1, Z - 1)], es_r.at[0])
    total = functools.reduce(jnp.add, [esum_in[z] for z in range(Z)])
    took(psum_in, ps_r.at[0])
    total = total + jnp.concatenate(
        [functools.reduce(jnp.add, [psum_in[half, z] for z in range(Z)]) for half in range(PARTS)], axis=0
    )
    total = dot(factor, total, NN, HIGH) * (1.0 / (DP * float(WIDTH) ** 0.5))
    red[...] = total.astype(BF16)
    start(ra_copy, RING8)
    qbuf[chunk(mz) * 2 + core] = red[...]
    fw_copy(0).start()

    for near in range(1, 5):
        pair = sorted({near, Z - near})
        took(qbuf.at[pl.ds(0, len(pair))], ra_r.at[near - 1])
        for k in pair:
            fw_copy(k).start()

    took(qbuf.at[pl.ds(0, Z)], fw_r.at[0])
    for p in range(DP):
        q_ref[:, p * CH : (p + 1) * CH] = qbuf[p].astype(F32)

    psum_like = psum.reshape(PARTS * Z, RH, CH)

    @pl.when(own_source)
    def _():
        took(psum_like.at[pl.ds(0, 7 * PARTS)], ps_s.at[0])

    @pl.when(jnp.logical_not(own_source))
    def _():
        took(psum_like, ps_s.at[0])

    took(qbuf.at[pl.ds(0, Z - 1)], ra_s.at[0])
    took(qbuf.at[pl.ds(0, Z)], fw_s.at[0])


def finish(p_in, q_in, p_out, q_out, sem):
    copies = [pltpu.make_async_copy(p_in, p_out, sem.at[0]), pltpu.make_async_copy(q_in, q_out.at[0], sem.at[1])]
    for copy in copies:
        copy.start()
    for copy in copies:
        copy.wait()


def shards(gate_pre, up_pre, grad_out, error, sketch):
    vmem = pltpu.VMEM
    dma = pltpu.SemaphoreType.DMA
    scratch = [
        vmem((TOK, WIDTH), BF16),
        vmem((TOK, WIDTH), BF16),
        vmem((TOK, 4 * LC), BF16),
        vmem((OWN, D), BF16),
        vmem((WIDTH, D), BF16),
        vmem((R, D), F32),
        vmem((2 * R, D), BF16),
        vmem((2, TENSOR, OWN, COLS), BF16),
        vmem((R, 2 * OWN), BF16),
        vmem((TENSOR, R, 2 * OWN), BF16),
        vmem((2 * R, TOK), BF16),
        vmem((DP, 8, LC), F32),
        vmem((Z, 8, LC), F32),
        vmem((Z, 8, LC), F32),
        vmem((8, LC), F32),
        vmem((DP, 8, LC), F32),
        vmem((R, 4 * LC), F32),
        vmem((PARTS, 2, 4, 2 * RH, TOK), BF16),
        vmem((2, Z, R, CH), F32),
        vmem((Z, R, CH), F32),
        vmem((Z, R, CH), F32),
        vmem((Z, R, CH), F32),
        vmem((PARTS, 2, 2, 4, RH, CH), F32),
        vmem((PARTS, 2, 4, RH, CH), F32),
        vmem((PARTS, Z, RH, CH), F32),
        vmem((PARTS, Z, RH, CH), F32),
        vmem((R, CH), BF16),
        vmem((DP, R, CH), BF16),
        dma((5,)),
        dma((1,)), dma((1,)),
        dma((1,)), dma((2,)),
        dma((1,)), dma((2,)),
        dma((1,)), dma((1,)),
        dma((1,)), dma((1,)),
        dma((1,)), dma((4,)),
        dma((1,)), dma((1,)),
        dma((1,)), dma((PARTS,)),
        dma((1,)), dma((Z // 2,)),
        dma((1,)), dma((1,)),
        dma((1,)), dma((PARTS,)),
        dma((1,)), dma((1,)),
        dma((1,)), dma((4,)),
        dma((1,)), dma((1,)),
    ]
    p_factor, q_factor = pl.pallas_call(
        kernel,
        out_shape=(pltpu.VMEM((R, WIDTH), F32), pltpu.VMEM((R, D), F32)),
        in_specs=[pl.BlockSpec(memory_space=pl.ANY)] * 5,
        out_specs=(pl.BlockSpec(memory_space=pltpu.VMEM), pl.BlockSpec(memory_space=pltpu.VMEM)),
        scratch_shapes=scratch,
        compiler_params=pltpu.CompilerParams(
            collective_id=0, has_side_effects=True, vmem_limit_bytes=56 * 1024 * 1024
        ),
    )(gate_pre, up_pre, grad_out, error[0], sketch)
    return pl.pallas_call(
        finish,
        out_shape=(jax.ShapeDtypeStruct((R, WIDTH), F32), jax.ShapeDtypeStruct((1, R, D), F32)),
        in_specs=[pl.BlockSpec(memory_space=pltpu.VMEM)] * 2,
        out_specs=(pl.BlockSpec(memory_space=pl.ANY), pl.BlockSpec(memory_space=pl.ANY)),
        scratch_shapes=[dma((2,))],
    )(pltpu.with_memory_space_constraint(p_factor, pltpu.VMEM), pltpu.with_memory_space_constraint(q_factor, pltpu.VMEM))


def solution(mesh):
    return jax.shard_map(
        shards,
        mesh=mesh,
        in_specs=(
            P("dp", "tensor"),
            P("dp", "tensor"),
            P(("dp", "tensor"), None),
            P("dp", "tensor", None),
            P(),
        ),
        out_specs=(P(None, "tensor"), P("tensor", None, None)),
        check_vma=False,
    )
```

```python
import functools

import jax
import jax.numpy as jnp
from jax import lax
from jax.experimental import pallas as pl
from jax.experimental.pallas import tpu as pltpu
from jax.sharding import PartitionSpec as P

MESH = pl.DeviceIdType.MESH
HIGH = lax.Precision.HIGHEST
F32 = jnp.float32
BF16 = jnp.bfloat16
NT = (((1,), (1,)), ((), ()))
NN = (((1,), (0,)), ((), ()))

D = 4096
WIDTH = 896
TOK = 1024
R = 32
HR = R // 2
PARTS = 4
RH = R // PARTS
DP = 16
TENSOR = 16
X = 4
Y = 4
Z = 8
OWN = 64
HALF = D // 2
COLS = HALF // 4
CH = D // DP
LC = 256
RING4 = (2, 1, 3)
RING8 = (4, 3, 5, 2, 6, 1, 7)
GRID = tuple(
    sorted(
        ((a, b) for a in range(X) for b in range(Y) if a or b),
        key=lambda k: -min(k[0], X - k[0]) - min(k[1], Y - k[1]),
    )
)
LAG = 3


def dot(a, b, dims=NN, precision=None):
    return lax.dot_general(a, b, dims, precision=precision, preferred_element_type=F32)


def split(value):
    high = value.astype(BF16)
    low = (value - high.astype(F32)).astype(BF16)
    return jnp.concatenate([high, low], axis=0)


def fold(product):
    half = product.shape[0] // 2
    return product[:half] + product[half:]


def inverse_factor(gram):
    rows = lax.broadcasted_iota(jnp.int32, (R, 128), 0)
    lanes = lax.broadcasted_iota(jnp.int32, (R, 128), 1)
    wide = jnp.concatenate([gram, jnp.zeros((R, 128 - R), F32)], axis=1)
    wide = jnp.where(lanes == rows + R, 1.0, wide)
    for k in range(R):
        factor = wide[:, k : k + 1] / wide[k : k + 1, k : k + 1]
        wide = wide - jnp.where(rows > k, factor * wide[k : k + 1, :], 0.0)
    pivots = jnp.sum(jnp.where(lanes == rows, wide, 0.0), axis=1, keepdims=True)
    return (wide * lax.rsqrt(pivots))[:, R : 2 * R]


def kernel(
    gate_hbm, up_hbm, g_hbm, e_hbm, sk_hbm,
    p_ref, q_ref,
    gate, up, hidden, g, e, sk, sks, gcols,
    proj, proj_in, proj_all, left, left_half, left_in, left_red, left_all, leftw,
    mix, errors, errors_in, esum, esum_in, part, part_in, psum, psum_in, red, qbuf,
    load_sem,
    proj_s, proj_r, gs_s, gs_r, gl_s, gl_r, lc_s, lc_r, ls_s, ls_r, la_s, la_r, lf_s, lf_r,
    mx_s, mx_r, ec_s, ec_r, es_s, es_r, pc_s, pc_r, ps_s, ps_r, ra_s, ra_r, fw_s, fw_r,
):
    dp = lax.axis_index("dp")
    tensor = lax.axis_index("tensor")
    mx = tensor // Y
    my = lax.rem(tensor, Y)
    mz = dp // 2
    core = lax.rem(dp, 2)

    barrier = pltpu.get_barrier_semaphore()

    def signal(peer):
        pl.semaphore_signal(barrier, inc=1, device_id=peer, device_id_type=MESH)

    for a, b in GRID:
        signal({"tensor": lax.rem(mx + a, X) * Y + lax.rem(my + b, Y)})

    def cols(half, place):
        return pl.ds(pl.multiple_of(half * HALF + place * COLS, COLS), COLS)

    loads = [
        pltpu.make_async_copy(sk_hbm, sk, load_sem.at[0]),
        pltpu.make_async_copy(g_hbm, g, load_sem.at[1]),
    ]
    for i in range(2):
        rows = pl.ds(i * TOK // 2, TOK // 2)
        loads.append(pltpu.make_async_copy(gate_hbm.at[rows], gate.at[rows], load_sem.at[2 + i]))
        loads.append(pltpu.make_async_copy(up_hbm.at[rows], up.at[rows], load_sem.at[2 + i]))
    spans = [(0, 512), (512, WIDTH)]
    error_loads = []
    for i, (at, to) in enumerate(spans):
        rows = pl.ds(at, to - at)
        error_loads.append(pltpu.make_async_copy(e_hbm.at[rows], e.at[rows], load_sem.at[4 + i]))
    loads += error_loads
    for load in loads:
        load.start()

    for k in RING8:
        for other in (core, 1 - core):
            signal({"dp": lax.rem(mz + k, Z) * 2 + other})
    signal({"dp": mz * 2 + 1 - core})

    block_y = lax.rem(my + Y - lax.rem(mz, Y), Y)
    block_x = lax.rem(mx + X - lax.rem(mz, X), X)
    source = jnp.where(mz < Y, mx * Y + block_y, block_x * Y + my)
    own_source = lax.rem(mz, Y) == 0
    for k in RING8:
        signal({"dp": lax.rem(mz + k, Z) * 2 + core, "tensor": source})

    @pl.when(jnp.logical_not(own_source))
    def _():
        signal({"dp": dp, "tensor": source})

    def remote(src, dst, send, recv, peer):
        return pltpu.make_async_remote_copy(
            src_ref=src, dst_ref=dst, send_sem=send, recv_sem=recv, device_id=peer, device_id_type=MESH
        )

    def y_peer(k):
        return {"tensor": mx * Y + lax.rem(my + k, Y)}

    def x_peer(k):
        return {"tensor": lax.rem(mx + k, X) * Y + my}

    def dp_peer(k):
        return {"dp": lax.rem(dp + k, DP)}

    def z_peer(k):
        return {"dp": lax.rem(mz + k, Z) * 2 + core}

    other_core = {"dp": mz * 2 + 1 - core}

    def proj_copy(k):
        return remote(
            proj, proj_in.at[tensor], proj_s.at[0], proj_r.at[0],
            {"tensor": lax.rem(mx + k[0], X) * Y + lax.rem(my + k[1], Y)},
        )

    def ga_copy(k):
        return remote(
            g.at[:, cols(0, lax.rem(my + k, Y))], gcols.at[0, tensor], gs_s.at[0], gs_r.at[0], y_peer(k)
        )

    def gb_copy(k):
        return remote(
            g.at[:, cols(1, lax.rem(mx + k, X))], gcols.at[1, tensor], gs_s.at[0], gs_r.at[1], x_peer(k)
        )

    def gax_copy(i, k):
        row = gcols.at[0, mx * Y + i]
        return remote(row, row, gl_s.at[0], gl_r.at[0], x_peer(k))

    def gby_copy(i, k):
        row = gcols.at[1, i * Y + my]
        return remote(row, row, gl_s.at[0], gl_r.at[1], y_peer(k))

    def own_a():
        return g.at[:, cols(0, my)], gcols.at[0, tensor]

    def own_b():
        return g.at[:, cols(1, mx)], gcols.at[1, tensor]

    def oax_copy(k):
        return remote(*own_a(), gl_s.at[0], gl_r.at[0], x_peer(k))

    def oby_copy(k):
        return remote(*own_b(), gl_s.at[0], gl_r.at[1], y_peer(k))

    def lc_copy():
        rows = left.at[pl.ds((1 - core) * Z, Z)]
        return remote(rows, left_half, lc_s.at[0], lc_r.at[0], other_core)

    def ls_copy(k):
        return remote(left.at[core * Z + lax.rem(mz + k, Z)], left_in.at[k], ls_s.at[0], ls_r.at[0], z_peer(k))

    def la_copy(k):
        return remote(left_red, left_all.at[core * Z + mz], la_s.at[0], la_r.at[min(k, Z - k) - 1], z_peer(k))

    def lf_copy(k):
        held = left_all.at[core * Z + lax.rem(mz + Z - k, Z)]
        return remote(held, held, lf_s.at[0], lf_r.at[0], other_core)

    def mix_copy(half, side, k):
        return remote(
            mix.at[half, 0, 0], mix.at[half, side, k], mx_s.at[0], mx_r.at[half],
            (y_peer, x_peer)[side](k),
        )

    def errors_copy(j):
        return remote(errors.at[1 - core, j], errors_in.at[j], ec_s.at[0], ec_r.at[j], other_core)

    def chunk(z):
        return jnp.where(z < Y, lax.rem(my + Y - lax.rem(z, Y), Y), Y + lax.rem(mx + X - lax.rem(z, X), X))

    def es_copy(n, z):
        return remote(esum.at[n], esum_in.at[mz], es_s.at[0], es_r.at[0], {"dp": z * 2 + core})

    def part_copy(half):
        return remote(part.at[half, 1 - core], part_in.at[half], pc_s.at[0], pc_r.at[half], other_core)

    def ps_copy(half, z):
        k = lax.rem(z, 4)
        there = jnp.where(z < 4, mx * Y + lax.rem(my + k, Y), lax.rem(mx + k, X) * Y + my)
        return remote(
            psum.at[half, z], psum_in.at[half, mz], ps_s.at[0], ps_r.at[half // 2], {"dp": z * 2 + core, "tensor": there}
        )

    def ra_copy(half, k):
        return remote(
            red.at[half], qbuf.at[half, chunk(mz) * 2 + core], ra_s.at[0], ra_r.at[half, min(k, Z - k) - 1], z_peer(k)
        )

    def fw_copy(half, k):
        held = qbuf.at[half, chunk(lax.rem(mz + Z - k, Z)) * 2 + core]
        return remote(held, held, fw_s.at[0], fw_r.at[half], other_core)

    def start(copy, order):
        for k in order:
            copy(k).start()

    def took(like, sem):
        pltpu.make_async_copy(like, like, sem).wait()

    loads[0].wait()
    sks[...] = split(sk[...])
    loads[1].wait()
    projected = fold(dot(sks[...], g[...], NT))
    high = projected.astype(BF16)
    low = (projected - high.astype(F32)).astype(BF16)
    proj[...] = jnp.concatenate([high, low], axis=1)
    proj_in[tensor] = proj[...]

    pl.semaphore_wait(barrier, TENSOR - 1 + DP - 1 + Z - own_source.astype(jnp.int32))
    start(proj_copy, GRID)
    start(ga_copy, RING4)
    start(gb_copy, RING4)

    start(oax_copy, RING4)
    start(oby_copy, RING4)
    pltpu.make_async_copy(*own_a(), gl_r.at[0]).start()
    pltpu.make_async_copy(*own_b(), gl_r.at[1]).start()

    for i in range(2):
        took(gate, load_sem.at[2 + i])

        @pl.loop(i * TOK // 128, (i + 1) * TOK // 128)
        def _(j):
            rows = pl.ds(pl.multiple_of(j * 64, 64), 64)
            v = 0.5 * gate[rows, :].astype(F32)
            u = up[rows, :].astype(F32)
            hidden[rows, :WIDTH] = ((v + v * jnp.tanh(v)) * u).astype(BF16)
            hidden[rows, WIDTH:] = jnp.zeros((64, 4 * LC - WIDTH), BF16)

    for load, (at, to) in zip(error_loads, spans):
        load.wait()
        leftw[:, at:to] = fold(dot(sks[...], e[at:to, :], NT))

    took(proj_in.at[pl.ds(1, TENSOR - 1)], proj_r.at[0])
    for j in range(TENSOR // 2):
        a = proj_in[2 * j]
        b = proj_in[2 * j + 1]
        proj_all[0:R, j * 128 : (j + 1) * 128] = jnp.concatenate([a[:, :OWN], b[:, :OWN]], axis=1)
        proj_all[R : 2 * R, j * 128 : (j + 1) * 128] = jnp.concatenate([a[:, OWN:], b[:, OWN:]], axis=1)
    mine = leftw[:, :WIDTH] + fold(dot(proj_all[...], hidden[:, :WIDTH]))
    mine = jnp.concatenate([mine, jnp.zeros((R, 4 * LC - WIDTH), F32)], axis=1)
    for p in range(DP):
        row, at = 8 * (p % Z // 2), 2 * LC * (p // Z) + LC * (p % 2)
        left[p] = mine[row : row + 8, at : at + LC]

    lc_copy().start()
    lc_copy().wait_recv()
    for j in range(Z):
        left[core * Z + j] += left_half[j]
    start(ls_copy, RING8)
    took(gcols.at[0, pl.ds(0, 3)], gs_r.at[0])
    for k in range(1, 4):
        start(functools.partial(gax_copy, lax.rem(my + Y - k, Y)), RING4)
    took(gcols.at[1, pl.ds(0, 3)], gs_r.at[1])
    for k in range(1, 4):
        start(functools.partial(gby_copy, lax.rem(mx + X - k, X)), RING4)

    took(left_in.at[pl.ds(1, Z - 1)], ls_r.at[0])
    left_red[...] = left[core * Z + mz] + functools.reduce(jnp.add, [left_in[k] for k in range(1, Z)])
    start(la_copy, RING8)
    left_all[core * Z + mz] = left_red[...]
    lf_copy(0).start()

    for near in range(1, 5):
        pair = sorted({near, Z - near})
        took(left_all.at[pl.ds(0, len(pair))], la_r.at[near - 1])
        for k in pair:
            lf_copy(k).start()

    def product_of(which):
        chunks = [left_all[which * Z + z] for z in range(Z)]
        value = jnp.concatenate(
            [jnp.concatenate(chunks[2 * i : 2 * i + 2], axis=1) for i in range(Z // 2)], axis=0
        )
        place = pl.ds(pl.multiple_of(which * 2 * LC, 2 * LC), 2 * LC)
        leftw[:, place] = value
        return fold(dot(split(value), hidden[:, place], NT))

    mixed = product_of(core)
    took(left_all.at[pl.ds(0, Z)], lf_r.at[0])
    mixed = mixed + product_of(1 - core)
    for half in range(PARTS):
        mix[half, 0, 0] = split(mixed[RH * half : RH * (half + 1)])
        for side in range(2):
            start(functools.partial(mix_copy, half, side), RING4)
    for half in range(PARTS):
        mix[half, 1, 0] = mix[half, 0, 0]

    whole = split(leftw[:, :WIDTH])

    def turn(n):
        away = (n + 1) // 2
        return lax.rem(mz + 4 + jnp.where(lax.rem(n, 2) == 0, away, Z - away), Z)

    @pl.loop(0, Z + LAG)
    def _(n):
        @pl.when(n < Z)
        def _():
            place = chunk(turn(n))
            for part_of in range(2):
                at = pl.multiple_of((2 * place + part_of) * CH, CH)
                errors[part_of, n] = fold(dot(whole, e[:, pl.ds(at, CH)]))
            errors_copy(n).start()

        @pl.when(n >= LAG)
        def _():
            i = n - LAG
            errors_copy(i).wait_recv()
            esum[i] = errors[core, i] + errors_in[i]

            @pl.when(i == Z - 1)
            def _():
                esum_in[mz] = esum[i]

            @pl.when(i != Z - 1)
            def _():
                es_copy(i, turn(i)).start()

    gcols_like = gcols.reshape(2 * TENSOR, OWN, COLS)
    mix_like = mix.reshape(PARTS * 2 * 4, 2 * RH, TOK)

    def product(half, side):
        rows = mix[half, side].reshape(4 * 2 * RH, TOK)
        for part_of in range(2):
            block = dot(rows, gcols[side, :, :, part_of * CH : (part_of + 1) * CH].reshape(TOK, CH))
            for k in range(4):
                part[half, part_of, side, (4 - k) % 4] = fold(block[2 * RH * k : 2 * RH * (k + 1)])

    def pieces(half):
        for side in range(2):
            for k in range(4):
                psum[half, 4 * side + k] = part[half, core, side, k] + part_in[half, side, k]
        for offset in RING8:
            ps_copy(half, lax.rem(mz + offset, Z)).start()

        @pl.when(own_source)
        def _():
            pltpu.make_async_copy(psum.at[half, mz], psum_in.at[half, mz], ps_r.at[half // 2]).start()

        @pl.when(jnp.logical_not(own_source))
        def _():
            ps_copy(half, mz).start()

    for side in range(2):
        took(gcols.at[side, pl.ds(0, 13)], gl_r.at[side])
    for half in range(PARTS + 1):
        if half < PARTS:
            took(mix_like.at[pl.ds(0, 6)], mx_r.at[half])
            for side in range(2):
                product(half, side)
            part_copy(half).start()
        if half > 0:
            part_copy(half - 1).wait_recv()
            pieces(half - 1)

    full = leftw[:, :WIDTH]
    factor = inverse_factor(dot(full, full, NT, HIGH))
    p_ref[...] = dot(factor, full, NN, HIGH) * (float(WIDTH) ** 0.5)
    took(proj_in.at[pl.ds(1, TENSOR - 1)], proj_s.at[0])
    took(gcols_like.at[pl.ds(0, 6)], gs_s.at[0])
    took(gcols_like.at[pl.ds(0, 24)], gl_s.at[0])
    took(mix_like.at[pl.ds(0, 6 * PARTS)], mx_s.at[0])
    lc_copy().wait_send()
    took(left_in.at[pl.ds(1, Z - 1)], ls_s.at[0])
    took(left_in.at[pl.ds(1, Z - 1)], la_s.at[0])
    took(left_in, lf_s.at[0])
    took(errors_in, ec_s.at[0])
    took(esum_in.at[pl.ds(1, Z - 1)], es_s.at[0])
    took(part_in, pc_s.at[0])

    took(esum_in.at[pl.ds(1, Z - 1)], es_r.at[0])
    total = functools.reduce(jnp.add, [esum_in[z] for z in range(Z)])

    sums = []
    for half in range(2):
        took(psum_in.at[pl.ds(2 * half, 2)], ps_r.at[half])
        for part_of in (2 * half, 2 * half + 1):
            sums.append(
                total[RH * part_of : RH * (part_of + 1)]
                + functools.reduce(jnp.add, [psum_in[part_of, z] for z in range(Z)])
            )
        to = HR * (half + 1)
        rows = dot(factor[HR * half : to, :to], jnp.concatenate(sums, axis=0), NN, HIGH)
        red[half] = (rows * (1.0 / (DP * float(WIDTH) ** 0.5))).astype(BF16)
        start(functools.partial(ra_copy, half), RING8)
        qbuf[half, chunk(mz) * 2 + core] = red[half]
        fw_copy(half, 0).start()
    for half in range(2):
        for near in range(1, 5):
            pair = sorted({near, Z - near})
            took(qbuf.at[half, pl.ds(0, len(pair))], ra_r.at[half, near - 1])
            for k in pair:
                fw_copy(half, k).start()
    for half in range(2):
        took(qbuf.at[half, pl.ds(0, Z)], fw_r.at[half])
        for p in range(DP):
            q_ref[HR * half : HR * (half + 1), p * CH : (p + 1) * CH] = qbuf[half, p].astype(F32)

    psum_like = psum.reshape(PARTS * Z, RH, CH)

    @pl.when(own_source)
    def _():
        took(psum_like.at[pl.ds(0, 7 * PARTS)], ps_s.at[0])

    @pl.when(jnp.logical_not(own_source))
    def _():
        took(psum_like, ps_s.at[0])

    took(qbuf.at[0, pl.ds(0, 2 * (Z - 1))], ra_s.at[0])
    took(qbuf.at[0], fw_s.at[0])


def finish(p_in, q_in, p_out, q_out, sem):
    copies = [pltpu.make_async_copy(p_in, p_out, sem.at[0]), pltpu.make_async_copy(q_in, q_out.at[0], sem.at[1])]
    for copy in copies:
        copy.start()
    for copy in copies:
        copy.wait()


def shards(gate_pre, up_pre, grad_out, error, sketch):
    vmem = pltpu.VMEM
    dma = pltpu.SemaphoreType.DMA
    scratch = [
        vmem((TOK, WIDTH), BF16),
        vmem((TOK, WIDTH), BF16),
        vmem((TOK, 4 * LC), BF16),
        vmem((OWN, D), BF16),
        vmem((WIDTH, D), BF16),
        vmem((R, D), F32),
        vmem((2 * R, D), BF16),
        vmem((2, TENSOR, OWN, COLS), BF16),
        vmem((R, 2 * OWN), BF16),
        vmem((TENSOR, R, 2 * OWN), BF16),
        vmem((2 * R, TOK), BF16),
        vmem((DP, 8, LC), F32),
        vmem((Z, 8, LC), F32),
        vmem((Z, 8, LC), F32),
        vmem((8, LC), F32),
        vmem((DP, 8, LC), F32),
        vmem((R, 4 * LC), F32),
        vmem((PARTS, 2, 4, 2 * RH, TOK), BF16),
        vmem((2, Z, R, CH), F32),
        vmem((Z, R, CH), F32),
        vmem((Z, R, CH), F32),
        vmem((Z, R, CH), F32),
        vmem((PARTS, 2, 2, 4, RH, CH), F32),
        vmem((PARTS, 2, 4, RH, CH), F32),
        vmem((PARTS, Z, RH, CH), F32),
        vmem((PARTS, Z, RH, CH), F32),
        vmem((2, HR, CH), BF16),
        vmem((2, DP, HR, CH), BF16),
        dma((6,)),
        dma((1,)), dma((1,)),
        dma((1,)), dma((2,)),
        dma((1,)), dma((2,)),
        dma((1,)), dma((1,)),
        dma((1,)), dma((1,)),
        dma((1,)), dma((4,)),
        dma((1,)), dma((1,)),
        dma((1,)), dma((PARTS,)),
        dma((1,)), dma((Z,)),
        dma((1,)), dma((1,)),
        dma((1,)), dma((PARTS,)),
        dma((1,)), dma((2,)),
        dma((1,)), dma((2, 4)),
        dma((1,)), dma((2,)),
    ]
    p_factor, q_factor = pl.pallas_call(
        kernel,
        out_shape=(pltpu.VMEM((R, WIDTH), F32), pltpu.VMEM((R, D), F32)),
        in_specs=[pl.BlockSpec(memory_space=pl.ANY)] * 5,
        out_specs=(pl.BlockSpec(memory_space=pltpu.VMEM), pl.BlockSpec(memory_space=pltpu.VMEM)),
        scratch_shapes=scratch,
        compiler_params=pltpu.CompilerParams(
            collective_id=0, has_side_effects=True, vmem_limit_bytes=56 * 1024 * 1024
        ),
    )(gate_pre, up_pre, grad_out, error[0], sketch)
    return pl.pallas_call(
        finish,
        out_shape=(jax.ShapeDtypeStruct((R, WIDTH), F32), jax.ShapeDtypeStruct((1, R, D), F32)),
        in_specs=[pl.BlockSpec(memory_space=pltpu.VMEM)] * 2,
        out_specs=(pl.BlockSpec(memory_space=pl.ANY), pl.BlockSpec(memory_space=pl.ANY)),
        scratch_shapes=[dma((2,))],
    )(pltpu.with_memory_space_constraint(p_factor, pltpu.VMEM), pltpu.with_memory_space_constraint(q_factor, pltpu.VMEM))


def solution(mesh):
    return jax.shard_map(
        shards,
        mesh=mesh,
        in_specs=(
            P("dp", "tensor"),
            P("dp", "tensor"),
            P(("dp", "tensor"), None),
            P("dp", "tensor", None),
            P(),
        ),
        out_specs=(P(None, "tensor"), P("tensor", None, None)),
        check_vma=False,
    )
```

```python
import functools

import jax
import jax.numpy as jnp
from jax import lax
from jax.experimental import pallas as pl
from jax.experimental.pallas import tpu as pltpu
from jax.sharding import PartitionSpec as P

MESH = pl.DeviceIdType.MESH
HIGH = lax.Precision.HIGHEST
F32 = jnp.float32
BF16 = jnp.bfloat16
NT = (((1,), (1,)), ((), ()))
NN = (((1,), (0,)), ((), ()))

D = 4096
WIDTH = 896
TOK = 1024
R = 32
HR = R // 2
PARTS = 4
RH = R // PARTS
DP = 16
TENSOR = 16
X = 4
Y = 4
Z = 8
OWN = 64
HALF = D // 2
COLS = HALF // 4
CH = D // DP
LC = 256
RING4 = (2, 1, 3)
RING8 = (4, 3, 5, 2, 6, 1, 7)
GRID = tuple(
    sorted(
        ((a, b) for a in range(X) for b in range(Y) if a or b),
        key=lambda k: -min(k[0], X - k[0]) - min(k[1], Y - k[1]),
    )
)
LAG = 2


def dot(a, b, dims=NN, precision=None):
    return lax.dot_general(a, b, dims, precision=precision, preferred_element_type=F32)


def split(value):
    high = value.astype(BF16)
    low = (value - high.astype(F32)).astype(BF16)
    return jnp.concatenate([high, low], axis=0)


def fold(product):
    half = product.shape[0] // 2
    return product[:half] + product[half:]


def inverse_factor(gram):
    rows = lax.broadcasted_iota(jnp.int32, (R, 128), 0)
    lanes = lax.broadcasted_iota(jnp.int32, (R, 128), 1)
    wide = jnp.concatenate([gram, jnp.zeros((R, 128 - R), F32)], axis=1)
    wide = jnp.where(lanes == rows + R, 1.0, wide)
    for k in range(R):
        factor = wide[:, k : k + 1] / wide[k : k + 1, k : k + 1]
        wide = wide - jnp.where(rows > k, factor * wide[k : k + 1, :], 0.0)
    pivots = jnp.sum(jnp.where(lanes == rows, wide, 0.0), axis=1, keepdims=True)
    return (wide * lax.rsqrt(pivots))[:, R : 2 * R]


def kernel(
    gate_hbm, up_hbm, g_hbm, e_hbm, sk_hbm,
    p_ref, q_ref,
    gate, up, hidden, g, e, sk, sks, gcols,
    proj, proj_in, proj_all, left, left_half, left_in, left_red, left_all, leftw,
    mix, errors, errors_in, esum, esum_in, part, part_in, psum, psum_in, red, qbuf,
    load_sem,
    proj_s, proj_r, gs_s, gs_r, gl_s, gl_r, lc_s, lc_r, ls_s, ls_r, la_s, la_r, lf_s, lf_r,
    mx_s, mx_r, ec_s, ec_r, es_s, es_r, pc_s, pc_r, ps_s, ps_r, ra_s, ra_r, fw_s, fw_r,
):
    dp = lax.axis_index("dp")
    tensor = lax.axis_index("tensor")
    mx = tensor // Y
    my = lax.rem(tensor, Y)
    mz = dp // 2
    core = lax.rem(dp, 2)

    barrier = pltpu.get_barrier_semaphore()

    def signal(peer):
        pl.semaphore_signal(barrier, inc=1, device_id=peer, device_id_type=MESH)

    for a, b in GRID:
        signal({"tensor": lax.rem(mx + a, X) * Y + lax.rem(my + b, Y)})

    def cols(half, place):
        return pl.ds(pl.multiple_of(half * HALF + place * COLS, COLS), COLS)

    loads = [
        pltpu.make_async_copy(sk_hbm, sk, load_sem.at[0]),
        pltpu.make_async_copy(g_hbm, g, load_sem.at[1]),
    ]
    for i in range(2):
        rows = pl.ds(i * TOK // 2, TOK // 2)
        loads.append(pltpu.make_async_copy(gate_hbm.at[rows], gate.at[rows], load_sem.at[2 + i]))
        loads.append(pltpu.make_async_copy(up_hbm.at[rows], up.at[rows], load_sem.at[2 + i]))
    spans = [(0, 512), (512, WIDTH)]
    error_loads = []
    for i, (at, to) in enumerate(spans):
        rows = pl.ds(at, to - at)
        error_loads.append(pltpu.make_async_copy(e_hbm.at[rows], e.at[rows], load_sem.at[4 + i]))
    loads += error_loads
    for load in loads:
        load.start()

    for k in RING8:
        for other in (core, 1 - core):
            signal({"dp": lax.rem(mz + k, Z) * 2 + other})
    signal({"dp": mz * 2 + 1 - core})

    block_y = lax.rem(my + Y - lax.rem(mz, Y), Y)
    block_x = lax.rem(mx + X - lax.rem(mz, X), X)
    source = jnp.where(mz < Y, mx * Y + block_y, block_x * Y + my)
    own_source = lax.rem(mz, Y) == 0
    for k in RING8:
        signal({"dp": lax.rem(mz + k, Z) * 2 + core, "tensor": source})

    @pl.when(jnp.logical_not(own_source))
    def _():
        signal({"dp": dp, "tensor": source})

    def remote(src, dst, send, recv, peer):
        return pltpu.make_async_remote_copy(
            src_ref=src, dst_ref=dst, send_sem=send, recv_sem=recv, device_id=peer, device_id_type=MESH
        )

    def y_peer(k):
        return {"tensor": mx * Y + lax.rem(my + k, Y)}

    def x_peer(k):
        return {"tensor": lax.rem(mx + k, X) * Y + my}

    def dp_peer(k):
        return {"dp": lax.rem(dp + k, DP)}

    def z_peer(k):
        return {"dp": lax.rem(mz + k, Z) * 2 + core}

    other_core = {"dp": mz * 2 + 1 - core}

    def proj_copy(k):
        return remote(
            proj, proj_in.at[tensor], proj_s.at[0], proj_r.at[0],
            {"tensor": lax.rem(mx + k[0], X) * Y + lax.rem(my + k[1], Y)},
        )

    def ga_copy(k):
        return remote(
            g.at[:, cols(0, lax.rem(my + k, Y))], gcols.at[0, tensor], gs_s.at[0], gs_r.at[0], y_peer(k)
        )

    def gb_copy(k):
        return remote(
            g.at[:, cols(1, lax.rem(mx + k, X))], gcols.at[1, tensor], gs_s.at[0], gs_r.at[1], x_peer(k)
        )

    def gax_copy(i, k):
        row = gcols.at[0, mx * Y + i]
        return remote(row, row, gl_s.at[0], gl_r.at[0], x_peer(k))

    def gby_copy(i, k):
        row = gcols.at[1, i * Y + my]
        return remote(row, row, gl_s.at[0], gl_r.at[1], y_peer(k))

    def own_a():
        return g.at[:, cols(0, my)], gcols.at[0, tensor]

    def own_b():
        return g.at[:, cols(1, mx)], gcols.at[1, tensor]

    def oax_copy(k):
        return remote(*own_a(), gl_s.at[0], gl_r.at[0], x_peer(k))

    def oby_copy(k):
        return remote(*own_b(), gl_s.at[0], gl_r.at[1], y_peer(k))

    def lc_copy():
        rows = left.at[pl.ds((1 - core) * Z, Z)]
        return remote(rows, left_half, lc_s.at[0], lc_r.at[0], other_core)

    def ls_copy(k):
        return remote(left.at[core * Z + lax.rem(mz + k, Z)], left_in.at[k], ls_s.at[0], ls_r.at[0], z_peer(k))

    def la_copy(k):
        return remote(left_red, left_all.at[core * Z + mz], la_s.at[0], la_r.at[min(k, Z - k) - 1], z_peer(k))

    def lf_copy(k):
        held = left_all.at[core * Z + lax.rem(mz + Z - k, Z)]
        return remote(held, held, lf_s.at[0], lf_r.at[0], other_core)

    def mix_copy(half, side, k):
        return remote(
            mix.at[half, 0, 0], mix.at[half, side, k], mx_s.at[0], mx_r.at[half],
            (y_peer, x_peer)[side](k),
        )

    def errors_copy(j):
        return remote(errors.at[1 - core, j], errors_in.at[j], ec_s.at[0], ec_r.at[j], other_core)

    def chunk(z):
        return jnp.where(z < Y, lax.rem(my + Y - lax.rem(z, Y), Y), Y + lax.rem(mx + X - lax.rem(z, X), X))

    def es_copy(n, z):
        return remote(esum.at[n], esum_in.at[mz], es_s.at[0], es_r.at[0], {"dp": z * 2 + core})

    def part_copy(half):
        return remote(part.at[half, 1 - core], part_in.at[half], pc_s.at[0], pc_r.at[half], other_core)

    def ps_copy(half, z):
        k = lax.rem(z, 4)
        there = jnp.where(z < 4, mx * Y + lax.rem(my + k, Y), lax.rem(mx + k, X) * Y + my)
        return remote(
            psum.at[half, z], psum_in.at[half, mz], ps_s.at[0], ps_r.at[half // 2], {"dp": z * 2 + core, "tensor": there}
        )

    def ra_copy(half, k):
        return remote(
            red.at[half], qbuf.at[half, chunk(mz) * 2 + core], ra_s.at[0], ra_r.at[half, min(k, Z - k) - 1], z_peer(k)
        )

    def fw_copy(half, k):
        held = qbuf.at[half, chunk(lax.rem(mz + Z - k, Z)) * 2 + core]
        return remote(held, held, fw_s.at[0], fw_r.at[half], other_core)

    def start(copy, order):
        for k in order:
            copy(k).start()

    def took(like, sem):
        pltpu.make_async_copy(like, like, sem).wait()

    loads[0].wait()
    sks[...] = split(sk[...])
    loads[1].wait()
    projected = fold(dot(sks[...], g[...], NT))
    high = projected.astype(BF16)
    low = (projected - high.astype(F32)).astype(BF16)
    proj[...] = jnp.concatenate([high, low], axis=1)
    proj_in[tensor] = proj[...]

    pl.semaphore_wait(barrier, TENSOR - 1 + DP - 1 + Z - own_source.astype(jnp.int32))
    start(proj_copy, GRID)


    for i in range(2):
        took(gate, load_sem.at[2 + i])

        @pl.loop(i * TOK // 128, (i + 1) * TOK // 128)
        def _(j):
            rows = pl.ds(pl.multiple_of(j * 64, 64), 64)
            v = 0.5 * gate[rows, :].astype(F32)
            u = up[rows, :].astype(F32)
            hidden[rows, :WIDTH] = ((v + v * jnp.tanh(v)) * u).astype(BF16)
            hidden[rows, WIDTH:] = jnp.zeros((64, 4 * LC - WIDTH), BF16)

    for load, (at, to) in zip(error_loads, spans):
        load.wait()
        leftw[:, at:to] = fold(dot(sks[...], e[at:to, :], NT))

    start(ga_copy, RING4)
    start(gb_copy, RING4)
    took(proj_in.at[pl.ds(1, TENSOR - 1)], proj_r.at[0])
    for j in range(TENSOR // 2):
        a = proj_in[2 * j]
        b = proj_in[2 * j + 1]
        proj_all[0:R, j * 128 : (j + 1) * 128] = jnp.concatenate([a[:, :OWN], b[:, :OWN]], axis=1)
        proj_all[R : 2 * R, j * 128 : (j + 1) * 128] = jnp.concatenate([a[:, OWN:], b[:, OWN:]], axis=1)
    mine = leftw[:, :WIDTH] + fold(dot(proj_all[...], hidden[:, :WIDTH]))
    mine = jnp.concatenate([mine, jnp.zeros((R, 4 * LC - WIDTH), F32)], axis=1)
    for p in range(DP):
        row, at = 8 * (p % Z // 2), 2 * LC * (p // Z) + LC * (p % 2)
        left[p] = mine[row : row + 8, at : at + LC]

    lc_copy().start()
    lc_copy().wait_recv()
    for j in range(Z):
        left[core * Z + j] += left_half[j]
    start(ls_copy, RING8)
    start(oax_copy, RING4)
    start(oby_copy, RING4)
    pltpu.make_async_copy(*own_a(), gl_r.at[0]).start()
    pltpu.make_async_copy(*own_b(), gl_r.at[1]).start()
    took(gcols.at[0, pl.ds(0, 3)], gs_r.at[0])
    for k in range(1, 4):
        start(functools.partial(gax_copy, lax.rem(my + Y - k, Y)), RING4)
    took(gcols.at[1, pl.ds(0, 3)], gs_r.at[1])
    for k in range(1, 4):
        start(functools.partial(gby_copy, lax.rem(mx + X - k, X)), RING4)

    took(left_in.at[pl.ds(1, Z - 1)], ls_r.at[0])
    left_red[...] = left[core * Z + mz] + functools.reduce(jnp.add, [left_in[k] for k in range(1, Z)])
    start(la_copy, RING8)
    left_all[core * Z + mz] = left_red[...]
    lf_copy(0).start()

    for near in range(1, 5):
        pair = sorted({near, Z - near})
        took(left_all.at[pl.ds(0, len(pair))], la_r.at[near - 1])
        for k in pair:
            lf_copy(k).start()

    def product_of(which):
        chunks = [left_all[which * Z + z] for z in range(Z)]
        value = jnp.concatenate(
            [jnp.concatenate(chunks[2 * i : 2 * i + 2], axis=1) for i in range(Z // 2)], axis=0
        )
        place = pl.ds(pl.multiple_of(which * 2 * LC, 2 * LC), 2 * LC)
        leftw[:, place] = value
        return fold(dot(split(value), hidden[:, place], NT))

    mixed = product_of(core)
    took(left_all.at[pl.ds(0, Z)], lf_r.at[0])
    mixed = mixed + product_of(1 - core)
    for half in range(PARTS):
        mix[half, 0, 0] = split(mixed[RH * half : RH * (half + 1)])
        for side in range(2):
            start(functools.partial(mix_copy, half, side), RING4)
    for half in range(PARTS):
        mix[half, 1, 0] = mix[half, 0, 0]

    whole = split(leftw[:, :WIDTH])

    def turn(n):
        away = (n + 1) // 2
        return lax.rem(mz + 4 + jnp.where(lax.rem(n, 2) == 0, away, Z - away), Z)

    @pl.loop(0, Z + LAG)
    def _(n):
        @pl.when(n < Z)
        def _():
            place = chunk(turn(n))
            for part_of in range(2):
                at = pl.multiple_of((2 * place + part_of) * CH, CH)
                errors[part_of, n] = fold(dot(whole, e[:, pl.ds(at, CH)]))
            errors_copy(n).start()

        @pl.when(n >= LAG)
        def _():
            i = n - LAG
            errors_copy(i).wait_recv()
            esum[i] = errors[core, i] + errors_in[i]

            @pl.when(i == Z - 1)
            def _():
                esum_in[mz] = esum[i]

            @pl.when(i != Z - 1)
            def _():
                es_copy(i, turn(i)).start()

    gcols_like = gcols.reshape(2 * TENSOR, OWN, COLS)
    mix_like = mix.reshape(PARTS * 2 * 4, 2 * RH, TOK)

    def product(half, side):
        rows = mix[half, side].reshape(4 * 2 * RH, TOK)
        for part_of in range(2):
            block = dot(rows, gcols[side, :, :, part_of * CH : (part_of + 1) * CH].reshape(TOK, CH))
            for k in range(4):
                part[half, part_of, side, (4 - k) % 4] = fold(block[2 * RH * k : 2 * RH * (k + 1)])

    def pieces(half):
        for side in range(2):
            for k in range(4):
                psum[half, 4 * side + k] = part[half, core, side, k] + part_in[half, side, k]
        for offset in RING8:
            ps_copy(half, lax.rem(mz + offset, Z)).start()

        @pl.when(own_source)
        def _():
            pltpu.make_async_copy(psum.at[half, mz], psum_in.at[half, mz], ps_r.at[half // 2]).start()

        @pl.when(jnp.logical_not(own_source))
        def _():
            ps_copy(half, mz).start()

    for side in range(2):
        took(gcols.at[side, pl.ds(0, 13)], gl_r.at[side])
    for half in range(PARTS + 1):
        if half < PARTS:
            took(mix_like.at[pl.ds(0, 6)], mx_r.at[half])
            for side in range(2):
                product(half, side)
            part_copy(half).start()
        if half > 0:
            part_copy(half - 1).wait_recv()
            pieces(half - 1)

    full = leftw[:, :WIDTH]
    factor = inverse_factor(dot(full, full, NT, HIGH))
    p_ref[...] = dot(factor, full, NN, HIGH) * (float(WIDTH) ** 0.5)
    took(proj_in.at[pl.ds(1, TENSOR - 1)], proj_s.at[0])
    took(gcols_like.at[pl.ds(0, 6)], gs_s.at[0])
    took(gcols_like.at[pl.ds(0, 24)], gl_s.at[0])
    took(mix_like.at[pl.ds(0, 6 * PARTS)], mx_s.at[0])
    lc_copy().wait_send()
    took(left_in.at[pl.ds(1, Z - 1)], ls_s.at[0])
    took(left_in.at[pl.ds(1, Z - 1)], la_s.at[0])
    took(left_in, lf_s.at[0])
    took(errors_in, ec_s.at[0])
    took(esum_in.at[pl.ds(1, Z - 1)], es_s.at[0])
    took(part_in, pc_s.at[0])

    took(esum_in.at[pl.ds(1, Z - 1)], es_r.at[0])
    total = functools.reduce(jnp.add, [esum_in[z] for z in range(Z)])

    sums = []
    for half in range(2):
        took(psum_in.at[pl.ds(2 * half, 2)], ps_r.at[half])
        for part_of in (2 * half, 2 * half + 1):
            sums.append(
                total[RH * part_of : RH * (part_of + 1)]
                + functools.reduce(jnp.add, [psum_in[part_of, z] for z in range(Z)])
            )
        to = HR * (half + 1)
        rows = dot(factor[HR * half : to, :to], jnp.concatenate(sums, axis=0), NN, HIGH)
        red[half] = (rows * (1.0 / (DP * float(WIDTH) ** 0.5))).astype(BF16)
        start(functools.partial(ra_copy, half), RING8)
        qbuf[half, chunk(mz) * 2 + core] = red[half]
        fw_copy(half, 0).start()
    for half in range(2):
        for near in range(1, 5):
            pair = sorted({near, Z - near})
            took(qbuf.at[half, pl.ds(0, len(pair))], ra_r.at[half, near - 1])
            for k in pair:
                fw_copy(half, k).start()
    for half in range(2):
        took(qbuf.at[half, pl.ds(0, Z)], fw_r.at[half])
        for p in range(DP):
            q_ref[HR * half : HR * (half + 1), p * CH : (p + 1) * CH] = qbuf[half, p].astype(F32)

    psum_like = psum.reshape(PARTS * Z, RH, CH)

    @pl.when(own_source)
    def _():
        took(psum_like.at[pl.ds(0, 7 * PARTS)], ps_s.at[0])

    @pl.when(jnp.logical_not(own_source))
    def _():
        took(psum_like, ps_s.at[0])

    took(qbuf.at[0, pl.ds(0, 2 * (Z - 1))], ra_s.at[0])
    took(qbuf.at[0], fw_s.at[0])


def finish(p_in, q_in, p_out, q_out, sem):
    copies = [pltpu.make_async_copy(p_in, p_out, sem.at[0]), pltpu.make_async_copy(q_in, q_out.at[0], sem.at[1])]
    for copy in copies:
        copy.start()
    for copy in copies:
        copy.wait()


def shards(gate_pre, up_pre, grad_out, error, sketch):
    vmem = pltpu.VMEM
    dma = pltpu.SemaphoreType.DMA
    scratch = [
        vmem((TOK, WIDTH), BF16),
        vmem((TOK, WIDTH), BF16),
        vmem((TOK, 4 * LC), BF16),
        vmem((OWN, D), BF16),
        vmem((WIDTH, D), BF16),
        vmem((R, D), F32),
        vmem((2 * R, D), BF16),
        vmem((2, TENSOR, OWN, COLS), BF16),
        vmem((R, 2 * OWN), BF16),
        vmem((TENSOR, R, 2 * OWN), BF16),
        vmem((2 * R, TOK), BF16),
        vmem((DP, 8, LC), F32),
        vmem((Z, 8, LC), F32),
        vmem((Z, 8, LC), F32),
        vmem((8, LC), F32),
        vmem((DP, 8, LC), F32),
        vmem((R, 4 * LC), F32),
        vmem((PARTS, 2, 4, 2 * RH, TOK), BF16),
        vmem((2, Z, R, CH), F32),
        vmem((Z, R, CH), F32),
        vmem((Z, R, CH), F32),
        vmem((Z, R, CH), F32),
        vmem((PARTS, 2, 2, 4, RH, CH), F32),
        vmem((PARTS, 2, 4, RH, CH), F32),
        vmem((PARTS, Z, RH, CH), F32),
        vmem((PARTS, Z, RH, CH), F32),
        vmem((2, HR, CH), BF16),
        vmem((2, DP, HR, CH), BF16),
        dma((6,)),
        dma((1,)), dma((1,)),
        dma((1,)), dma((2,)),
        dma((1,)), dma((2,)),
        dma((1,)), dma((1,)),
        dma((1,)), dma((1,)),
        dma((1,)), dma((4,)),
        dma((1,)), dma((1,)),
        dma((1,)), dma((PARTS,)),
        dma((1,)), dma((Z,)),
        dma((1,)), dma((1,)),
        dma((1,)), dma((PARTS,)),
        dma((1,)), dma((2,)),
        dma((1,)), dma((2, 4)),
        dma((1,)), dma((2,)),
    ]
    p_factor, q_factor = pl.pallas_call(
        kernel,
        out_shape=(pltpu.VMEM((R, WIDTH), F32), pltpu.VMEM((R, D), F32)),
        in_specs=[pl.BlockSpec(memory_space=pl.ANY)] * 5,
        out_specs=(pl.BlockSpec(memory_space=pltpu.VMEM), pl.BlockSpec(memory_space=pltpu.VMEM)),
        scratch_shapes=scratch,
        compiler_params=pltpu.CompilerParams(
            collective_id=0, has_side_effects=True, vmem_limit_bytes=56 * 1024 * 1024
        ),
    )(gate_pre, up_pre, grad_out, error[0], sketch)
    return pl.pallas_call(
        finish,
        out_shape=(jax.ShapeDtypeStruct((R, WIDTH), F32), jax.ShapeDtypeStruct((1, R, D), F32)),
        in_specs=[pl.BlockSpec(memory_space=pltpu.VMEM)] * 2,
        out_specs=(pl.BlockSpec(memory_space=pl.ANY), pl.BlockSpec(memory_space=pl.ANY)),
        scratch_shapes=[dma((2,))],
    )(pltpu.with_memory_space_constraint(p_factor, pltpu.VMEM), pltpu.with_memory_space_constraint(q_factor, pltpu.VMEM))


def solution(mesh):
    return jax.shard_map(
        shards,
        mesh=mesh,
        in_specs=(
            P("dp", "tensor"),
            P("dp", "tensor"),
            P(("dp", "tensor"), None),
            P("dp", "tensor", None),
            P(),
        ),
        out_specs=(P(None, "tensor"), P("tensor", None, None)),
        check_vma=False,
    )
```

```python
import functools

import jax
import jax.numpy as jnp
from jax import lax
from jax.experimental import pallas as pl
from jax.experimental.pallas import tpu as pltpu
from jax.sharding import PartitionSpec as P

MESH = pl.DeviceIdType.MESH
HIGH = lax.Precision.HIGHEST
F32 = jnp.float32
BF16 = jnp.bfloat16
NT = (((1,), (1,)), ((), ()))
NN = (((1,), (0,)), ((), ()))

D = 4096
WIDTH = 896
TOK = 1024
R = 32
HR = R // 2
PARTS = 4
RH = R // PARTS
DP = 16
TENSOR = 16
X = 4
Y = 4
Z = 8
OWN = 64
HALF = D // 2
COLS = HALF // 4
CH = D // DP
LC = 256
RING4 = (2, 1, 3)
RING8 = (4, 3, 5, 2, 6, 1, 7)
GRID = tuple(
    sorted(
        ((a, b) for a in range(X) for b in range(Y) if a or b),
        key=lambda k: -min(k[0], X - k[0]) - min(k[1], Y - k[1]),
    )
)
LAG = 2


def dot(a, b, dims=NN, precision=None):
    return lax.dot_general(a, b, dims, precision=precision, preferred_element_type=F32)


def split(value):
    high = value.astype(BF16)
    low = (value - high.astype(F32)).astype(BF16)
    return jnp.concatenate([high, low], axis=0)


def fold(product):
    half = product.shape[0] // 2
    return product[:half] + product[half:]


def inverse_factor(gram):
    rows = lax.broadcasted_iota(jnp.int32, (R, 128), 0)
    lanes = lax.broadcasted_iota(jnp.int32, (R, 128), 1)
    wide = jnp.concatenate([gram, jnp.zeros((R, 128 - R), F32)], axis=1)
    wide = jnp.where(lanes == rows + R, 1.0, wide)
    for k in range(R):
        factor = wide[:, k : k + 1] / wide[k : k + 1, k : k + 1]
        wide = wide - jnp.where(rows > k, factor * wide[k : k + 1, :], 0.0)
    pivots = jnp.sum(jnp.where(lanes == rows, wide, 0.0), axis=1, keepdims=True)
    return (wide * lax.rsqrt(pivots))[:, R : 2 * R]


def kernel(
    gate_hbm, up_hbm, g_hbm, e_hbm, sk_hbm,
    p_ref, q_ref,
    gate, up, hidden, g, e, sk, sks, gcols,
    proj, proj_in, proj_all, left, left_half, left_in, left_red, left_all, leftw,
    mix, errors, errors_in, esum, esum_in, part, part_in, psum, psum_in, red, qbuf,
    load_sem,
    proj_s, proj_r, gs_s, gs_r, gl_s, gl_r, lc_s, lc_r, ls_s, ls_r, la_s, la_r, lf_s, lf_r,
    mx_s, mx_r, ec_s, ec_r, es_s, es_r, pc_s, pc_r, ps_s, ps_r, ra_s, ra_r, fw_s, fw_r,
):
    dp = lax.axis_index("dp")
    tensor = lax.axis_index("tensor")
    mx = tensor // Y
    my = lax.rem(tensor, Y)
    mz = dp // 2
    core = lax.rem(dp, 2)

    barrier = pltpu.get_barrier_semaphore()

    def signal(peer):
        pl.semaphore_signal(barrier, inc=1, device_id=peer, device_id_type=MESH)

    for a, b in GRID:
        signal({"tensor": lax.rem(mx + a, X) * Y + lax.rem(my + b, Y)})

    def cols(half, place):
        return pl.ds(pl.multiple_of(half * HALF + place * COLS, COLS), COLS)

    loads = [
        pltpu.make_async_copy(sk_hbm, sk, load_sem.at[0]),
        pltpu.make_async_copy(g_hbm, g, load_sem.at[1]),
    ]
    for i in range(2):
        rows = pl.ds(i * TOK // 2, TOK // 2)
        loads.append(pltpu.make_async_copy(gate_hbm.at[rows], gate.at[rows], load_sem.at[2 + i]))
        loads.append(pltpu.make_async_copy(up_hbm.at[rows], up.at[rows], load_sem.at[2 + i]))
    spans = [(0, 512), (512, WIDTH)]
    error_loads = []
    for i, (at, to) in enumerate(spans):
        rows = pl.ds(at, to - at)
        error_loads.append(pltpu.make_async_copy(e_hbm.at[rows], e.at[rows], load_sem.at[4 + i]))
    loads += error_loads
    for load in loads:
        load.start()

    for k in RING8:
        for other in (core, 1 - core):
            signal({"dp": lax.rem(mz + k, Z) * 2 + other})
    signal({"dp": mz * 2 + 1 - core})

    block_y = lax.rem(my + Y - lax.rem(mz, Y), Y)
    block_x = lax.rem(mx + X - lax.rem(mz, X), X)
    source = jnp.where(mz < Y, mx * Y + block_y, block_x * Y + my)
    own_source = lax.rem(mz, Y) == 0
    for k in RING8:
        signal({"dp": lax.rem(mz + k, Z) * 2 + core, "tensor": source})

    @pl.when(jnp.logical_not(own_source))
    def _():
        signal({"dp": dp, "tensor": source})

    def remote(src, dst, send, recv, peer):
        return pltpu.make_async_remote_copy(
            src_ref=src, dst_ref=dst, send_sem=send, recv_sem=recv, device_id=peer, device_id_type=MESH
        )

    def y_peer(k):
        return {"tensor": mx * Y + lax.rem(my + k, Y)}

    def x_peer(k):
        return {"tensor": lax.rem(mx + k, X) * Y + my}

    def dp_peer(k):
        return {"dp": lax.rem(dp + k, DP)}

    def z_peer(k):
        return {"dp": lax.rem(mz + k, Z) * 2 + core}

    other_core = {"dp": mz * 2 + 1 - core}

    def proj_copy(k):
        return remote(
            proj, proj_in.at[tensor], proj_s.at[0], proj_r.at[0],
            {"tensor": lax.rem(mx + k[0], X) * Y + lax.rem(my + k[1], Y)},
        )

    def ga_copy(k):
        return remote(
            g.at[:, cols(0, lax.rem(my + k, Y))], gcols.at[0, tensor], gs_s.at[0], gs_r.at[0], y_peer(k)
        )

    def gb_copy(k):
        return remote(
            g.at[:, cols(1, lax.rem(mx + k, X))], gcols.at[1, tensor], gs_s.at[0], gs_r.at[1], x_peer(k)
        )

    def gax_copy(i, k):
        row = gcols.at[0, mx * Y + i]
        return remote(row, row, gl_s.at[0], gl_r.at[0], x_peer(k))

    def gby_copy(i, k):
        row = gcols.at[1, i * Y + my]
        return remote(row, row, gl_s.at[0], gl_r.at[1], y_peer(k))

    def own_a():
        return g.at[:, cols(0, my)], gcols.at[0, tensor]

    def own_b():
        return g.at[:, cols(1, mx)], gcols.at[1, tensor]

    def oax_copy(k):
        return remote(*own_a(), gl_s.at[0], gl_r.at[0], x_peer(k))

    def oby_copy(k):
        return remote(*own_b(), gl_s.at[0], gl_r.at[1], y_peer(k))

    def lc_copy():
        rows = left.at[pl.ds((1 - core) * Z, Z)]
        return remote(rows, left_half, lc_s.at[0], lc_r.at[0], other_core)

    def ls_copy(k):
        return remote(left.at[core * Z + lax.rem(mz + k, Z)], left_in.at[k], ls_s.at[0], ls_r.at[0], z_peer(k))

    def la_copy(k):
        return remote(left_red, left_all.at[core * Z + mz], la_s.at[0], la_r.at[min(k, Z - k) - 1], z_peer(k))

    def lf_copy(k):
        held = left_all.at[core * Z + lax.rem(mz + Z - k, Z)]
        return remote(held, held, lf_s.at[0], lf_r.at[0], other_core)

    def mix_copy(half, side, k):
        return remote(
            mix.at[half, 0, 0], mix.at[half, side, k], mx_s.at[0], mx_r.at[half],
            (y_peer, x_peer)[side](k),
        )

    def errors_copy(j):
        return remote(errors.at[1 - core, j], errors_in.at[j], ec_s.at[0], ec_r.at[j], other_core)

    def chunk(z):
        return jnp.where(z < Y, lax.rem(my + Y - lax.rem(z, Y), Y), Y + lax.rem(mx + X - lax.rem(z, X), X))

    def es_copy(n, z):
        return remote(esum.at[n], esum_in.at[mz], es_s.at[0], es_r.at[0], {"dp": z * 2 + core})

    def part_copy(half):
        return remote(part.at[half, 1 - core], part_in.at[half], pc_s.at[0], pc_r.at[half], other_core)

    def ps_copy(half, z):
        k = lax.rem(z, 4)
        there = jnp.where(z < 4, mx * Y + lax.rem(my + k, Y), lax.rem(mx + k, X) * Y + my)
        return remote(
            psum.at[half, z], psum_in.at[half, mz], ps_s.at[0], ps_r.at[half // 2], {"dp": z * 2 + core, "tensor": there}
        )

    def ra_copy(half, k):
        return remote(
            red.at[half], qbuf.at[half, chunk(mz) * 2 + core], ra_s.at[0], ra_r.at[half, min(k, Z - k) - 1], z_peer(k)
        )

    def fw_copy(half, k):
        held = qbuf.at[half, chunk(lax.rem(mz + Z - k, Z)) * 2 + core]
        return remote(held, held, fw_s.at[0], fw_r.at[half], other_core)

    def start(copy, order):
        for k in order:
            copy(k).start()

    def took(like, sem):
        pltpu.make_async_copy(like, like, sem).wait()

    loads[0].wait()
    sks[...] = split(sk[...])
    loads[1].wait()
    projected = fold(dot(sks[...], g[...], NT))
    high = projected.astype(BF16)
    low = (projected - high.astype(F32)).astype(BF16)
    proj[...] = jnp.concatenate([high, low], axis=1)
    proj_in[tensor] = proj[...]

    pl.semaphore_wait(barrier, TENSOR - 1 + DP - 1 + Z - own_source.astype(jnp.int32))
    start(proj_copy, GRID)


    for i in range(2):
        took(gate, load_sem.at[2 + i])

        @pl.loop(i * TOK // 128, (i + 1) * TOK // 128)
        def _(j):
            rows = pl.ds(pl.multiple_of(j * 64, 64), 64)
            v = 0.5 * gate[rows, :].astype(F32)
            u = up[rows, :].astype(F32)
            hidden[rows, :WIDTH] = ((v + v * jnp.tanh(v)) * u).astype(BF16)
            hidden[rows, WIDTH:] = jnp.zeros((64, 4 * LC - WIDTH), BF16)

    for load, (at, to) in zip(error_loads, spans):
        load.wait()
        leftw[:, at:to] = fold(dot(sks[...], e[at:to, :], NT))

    for k in RING4:
        ga_copy(k).start()
        gb_copy(k).start()
    took(proj_in.at[pl.ds(1, TENSOR - 1)], proj_r.at[0])
    for j in range(TENSOR // 2):
        a = proj_in[2 * j]
        b = proj_in[2 * j + 1]
        proj_all[0:R, j * 128 : (j + 1) * 128] = jnp.concatenate([a[:, :OWN], b[:, :OWN]], axis=1)
        proj_all[R : 2 * R, j * 128 : (j + 1) * 128] = jnp.concatenate([a[:, OWN:], b[:, OWN:]], axis=1)
    mine = leftw[:, :WIDTH] + fold(dot(proj_all[...], hidden[:, :WIDTH]))
    mine = jnp.concatenate([mine, jnp.zeros((R, 4 * LC - WIDTH), F32)], axis=1)
    for p in range(DP):
        row, at = 8 * (p % Z // 2), 2 * LC * (p // Z) + LC * (p % 2)
        left[p] = mine[row : row + 8, at : at + LC]

    lc_copy().start()
    lc_copy().wait_recv()
    for k in RING8 + (0,):
        there = lax.rem(mz + k, Z)
        left[core * Z + there] += left_half[there]
        if k:
            ls_copy(k).start()
    for k in RING4:
        oax_copy(k).start()
        oby_copy(k).start()
    pltpu.make_async_copy(*own_a(), gl_r.at[0]).start()
    pltpu.make_async_copy(*own_b(), gl_r.at[1]).start()
    took(gcols.at[0, pl.ds(0, 3)], gs_r.at[0])
    for k in range(1, 4):
        start(functools.partial(gax_copy, lax.rem(my + Y - k, Y)), RING4)
    took(gcols.at[1, pl.ds(0, 3)], gs_r.at[1])
    for k in range(1, 4):
        start(functools.partial(gby_copy, lax.rem(mx + X - k, X)), RING4)

    took(left_in.at[pl.ds(1, Z - 1)], ls_r.at[0])
    left_red[...] = left[core * Z + mz] + functools.reduce(jnp.add, [left_in[k] for k in range(1, Z)])
    start(la_copy, RING8)
    left_all[core * Z + mz] = left_red[...]
    lf_copy(0).start()

    for near in range(1, 5):
        pair = sorted({near, Z - near})
        took(left_all.at[pl.ds(0, len(pair))], la_r.at[near - 1])
        for k in pair:
            lf_copy(k).start()

    def product_of(which):
        chunks = [left_all[which * Z + z] for z in range(Z)]
        value = jnp.concatenate(
            [jnp.concatenate(chunks[2 * i : 2 * i + 2], axis=1) for i in range(Z // 2)], axis=0
        )
        place = pl.ds(pl.multiple_of(which * 2 * LC, 2 * LC), 2 * LC)
        leftw[:, place] = value
        return fold(dot(split(value), hidden[:, place], NT))

    mixed = product_of(core)
    took(left_all.at[pl.ds(0, Z)], lf_r.at[0])
    mixed = mixed + product_of(1 - core)
    for half in range(PARTS):
        mix[half, 0, 0] = split(mixed[RH * half : RH * (half + 1)])
        for k in RING4:
            for side in range(2):
                mix_copy(half, side, k).start()
    for half in range(PARTS):
        mix[half, 1, 0] = mix[half, 0, 0]

    whole = split(leftw[:, :WIDTH])

    def turn(n):
        away = (n + 1) // 2
        return lax.rem(mz + 4 + jnp.where(lax.rem(n, 2) == 0, away, Z - away), Z)

    @pl.loop(0, Z + LAG)
    def _(n):
        @pl.when(n < Z)
        def _():
            place = chunk(turn(n))
            for part_of in range(2):
                at = pl.multiple_of((2 * place + part_of) * CH, CH)
                errors[part_of, n] = fold(dot(whole, e[:, pl.ds(at, CH)]))
            errors_copy(n).start()

        @pl.when(n >= LAG)
        def _():
            i = n - LAG
            errors_copy(i).wait_recv()
            esum[i] = errors[core, i] + errors_in[i]

            @pl.when(i == Z - 1)
            def _():
                esum_in[mz] = esum[i]

            @pl.when(i != Z - 1)
            def _():
                es_copy(i, turn(i)).start()

    gcols_like = gcols.reshape(2 * TENSOR, OWN, COLS)
    mix_like = mix.reshape(PARTS * 2 * 4, 2 * RH, TOK)

    def product(half, side):
        rows = mix[half, side].reshape(4 * 2 * RH, TOK)
        for part_of in range(2):
            block = dot(rows, gcols[side, :, :, part_of * CH : (part_of + 1) * CH].reshape(TOK, CH))
            for k in range(4):
                part[half, part_of, side, (4 - k) % 4] = fold(block[2 * RH * k : 2 * RH * (k + 1)])

    def pieces(half):
        for offset in RING8 + (0,):
            z = lax.rem(mz + offset, Z)
            side, k = z // 4, lax.rem(z, 4)
            psum[half, z] = part[half, core, side, k] + part_in[half, side, k]
            if offset:
                ps_copy(half, z).start()

        @pl.when(own_source)
        def _():
            pltpu.make_async_copy(psum.at[half, mz], psum_in.at[half, mz], ps_r.at[half // 2]).start()

        @pl.when(jnp.logical_not(own_source))
        def _():
            ps_copy(half, mz).start()

    for side in range(2):
        took(gcols.at[side, pl.ds(0, 13)], gl_r.at[side])
    for half in range(PARTS + 1):
        if half < PARTS:
            took(mix_like.at[pl.ds(0, 6)], mx_r.at[half])
            for side in range(2):
                product(half, side)
            part_copy(half).start()
        if half > 0:
            part_copy(half - 1).wait_recv()
            pieces(half - 1)

    full = leftw[:, :WIDTH]
    factor = inverse_factor(dot(full, full, NT, HIGH))
    p_ref[...] = dot(factor, full, NN, HIGH) * (float(WIDTH) ** 0.5)
    took(proj_in.at[pl.ds(1, TENSOR - 1)], proj_s.at[0])
    took(gcols_like.at[pl.ds(0, 6)], gs_s.at[0])
    took(gcols_like.at[pl.ds(0, 24)], gl_s.at[0])
    took(mix_like.at[pl.ds(0, 6 * PARTS)], mx_s.at[0])
    lc_copy().wait_send()
    took(left_in.at[pl.ds(1, Z - 1)], ls_s.at[0])
    took(left_in.at[pl.ds(1, Z - 1)], la_s.at[0])
    took(left_in, lf_s.at[0])
    took(errors_in, ec_s.at[0])
    took(esum_in.at[pl.ds(1, Z - 1)], es_s.at[0])
    took(part_in, pc_s.at[0])

    took(esum_in.at[pl.ds(1, Z - 1)], es_r.at[0])
    total = functools.reduce(jnp.add, [esum_in[z] for z in range(Z)])

    sums = []
    for half in range(2):
        took(psum_in.at[pl.ds(2 * half, 2)], ps_r.at[half])
        for part_of in (2 * half, 2 * half + 1):
            sums.append(
                total[RH * part_of : RH * (part_of + 1)]
                + functools.reduce(jnp.add, [psum_in[part_of, z] for z in range(Z)])
            )
        to = HR * (half + 1)
        rows = dot(factor[HR * half : to, :to], jnp.concatenate(sums, axis=0), NN, HIGH)
        red[half] = (rows * (1.0 / (DP * float(WIDTH) ** 0.5))).astype(BF16)
        start(functools.partial(ra_copy, half), RING8)
        qbuf[half, chunk(mz) * 2 + core] = red[half]
        fw_copy(half, 0).start()
    for half in range(2):
        for near in range(1, 5):
            pair = sorted({near, Z - near})
            took(qbuf.at[half, pl.ds(0, len(pair))], ra_r.at[half, near - 1])
            for k in pair:
                fw_copy(half, k).start()
    for half in range(2):
        took(qbuf.at[half, pl.ds(0, Z)], fw_r.at[half])
        for p in range(DP):
            q_ref[HR * half : HR * (half + 1), p * CH : (p + 1) * CH] = qbuf[half, p].astype(F32)

    psum_like = psum.reshape(PARTS * Z, RH, CH)

    @pl.when(own_source)
    def _():
        took(psum_like.at[pl.ds(0, 7 * PARTS)], ps_s.at[0])

    @pl.when(jnp.logical_not(own_source))
    def _():
        took(psum_like, ps_s.at[0])

    took(qbuf.at[0, pl.ds(0, 2 * (Z - 1))], ra_s.at[0])
    took(qbuf.at[0], fw_s.at[0])


def finish(p_in, q_in, p_out, q_out, sem):
    copies = [pltpu.make_async_copy(p_in, p_out, sem.at[0]), pltpu.make_async_copy(q_in, q_out.at[0], sem.at[1])]
    for copy in copies:
        copy.start()
    for copy in copies:
        copy.wait()


def shards(gate_pre, up_pre, grad_out, error, sketch):
    vmem = pltpu.VMEM
    dma = pltpu.SemaphoreType.DMA
    scratch = [
        vmem((TOK, WIDTH), BF16),
        vmem((TOK, WIDTH), BF16),
        vmem((TOK, 4 * LC), BF16),
        vmem((OWN, D), BF16),
        vmem((WIDTH, D), BF16),
        vmem((R, D), F32),
        vmem((2 * R, D), BF16),
        vmem((2, TENSOR, OWN, COLS), BF16),
        vmem((R, 2 * OWN), BF16),
        vmem((TENSOR, R, 2 * OWN), BF16),
        vmem((2 * R, TOK), BF16),
        vmem((DP, 8, LC), F32),
        vmem((Z, 8, LC), F32),
        vmem((Z, 8, LC), F32),
        vmem((8, LC), F32),
        vmem((DP, 8, LC), F32),
        vmem((R, 4 * LC), F32),
        vmem((PARTS, 2, 4, 2 * RH, TOK), BF16),
        vmem((2, Z, R, CH), F32),
        vmem((Z, R, CH), F32),
        vmem((Z, R, CH), F32),
        vmem((Z, R, CH), F32),
        vmem((PARTS, 2, 2, 4, RH, CH), F32),
        vmem((PARTS, 2, 4, RH, CH), F32),
        vmem((PARTS, Z, RH, CH), F32),
        vmem((PARTS, Z, RH, CH), F32),
        vmem((2, HR, CH), BF16),
        vmem((2, DP, HR, CH), BF16),
        dma((6,)),
        dma((1,)), dma((1,)),
        dma((1,)), dma((2,)),
        dma((1,)), dma((2,)),
        dma((1,)), dma((1,)),
        dma((1,)), dma((1,)),
        dma((1,)), dma((4,)),
        dma((1,)), dma((1,)),
        dma((1,)), dma((PARTS,)),
        dma((1,)), dma((Z,)),
        dma((1,)), dma((1,)),
        dma((1,)), dma((PARTS,)),
        dma((1,)), dma((2,)),
        dma((1,)), dma((2, 4)),
        dma((1,)), dma((2,)),
    ]
    p_factor, q_factor = pl.pallas_call(
        kernel,
        out_shape=(pltpu.VMEM((R, WIDTH), F32), pltpu.VMEM((R, D), F32)),
        in_specs=[pl.BlockSpec(memory_space=pl.ANY)] * 5,
        out_specs=(pl.BlockSpec(memory_space=pltpu.VMEM), pl.BlockSpec(memory_space=pltpu.VMEM)),
        scratch_shapes=scratch,
        compiler_params=pltpu.CompilerParams(
            collective_id=0, has_side_effects=True, vmem_limit_bytes=56 * 1024 * 1024
        ),
    )(gate_pre, up_pre, grad_out, error[0], sketch)
    return pl.pallas_call(
        finish,
        out_shape=(jax.ShapeDtypeStruct((R, WIDTH), F32), jax.ShapeDtypeStruct((1, R, D), F32)),
        in_specs=[pl.BlockSpec(memory_space=pltpu.VMEM)] * 2,
        out_specs=(pl.BlockSpec(memory_space=pl.ANY), pl.BlockSpec(memory_space=pl.ANY)),
        scratch_shapes=[dma((2,))],
    )(pltpu.with_memory_space_constraint(p_factor, pltpu.VMEM), pltpu.with_memory_space_constraint(q_factor, pltpu.VMEM))


def solution(mesh):
    return jax.shard_map(
        shards,
        mesh=mesh,
        in_specs=(
            P("dp", "tensor"),
            P("dp", "tensor"),
            P(("dp", "tensor"), None),
            P("dp", "tensor", None),
            P(),
        ),
        out_specs=(P(None, "tensor"), P("tensor", None, None)),
        check_vma=False,
    )
```
